512 devices in a mesh: expert: 8 (over x, core), tensor: 64 (over y, z).
Axes of the slice: x: 4, y: 4, z: 16, core: 2. Of those that a mesh axis runs over, the one named last changes fastest.
Arguments:
- tokens: bfloat16 [256, 6144], P('expert', 'tensor'), may hold values from -6 to 6
- upstream: bfloat16 [256, 6144], P('expert', 'tensor'), may hold values from -3 to 3
- expert_ids: int32 [256, 2], P('expert'), may hold values from 0 to 7, as said below
- slot_pos: int32 [256, 2], P('expert'), may hold values from 0 to 20, as said below
- combine: float32 [256, 2], P('expert'), may hold values from 0.1 to 1
- gate_weight: bfloat16 [8, 6144, 8192], P('expert', None, 'tensor'), may hold values from -0.078125 to 0.078125
- upward_weight: bfloat16 [8, 6144, 8192], P('expert', None, 'tensor'), may hold values from -0.078125 to 0.078125
- down_weight: bfloat16 [8, 8192, 6144], P('expert', 'tensor'), may hold values from -0.0625 to 0.0625
- gate_adapter_first: bfloat16 [8, 6144, 16], P('expert', 'tensor'), may hold values from -0.078125 to 0.078125
- gate_adapter_second: bfloat16 [8, 16, 8192], P('expert', None, 'tensor'), may hold values from -0.29882812 to 0.29882812
- upward_adapter_first: bfloat16 [8, 6144, 16], P('expert', 'tensor'), may hold values from -0.078125 to 0.078125
- upward_adapter_second: bfloat16 [8, 16, 8192], P('expert', None, 'tensor'), may hold values from -0.29882812 to 0.29882812
- down_adapter_first: bfloat16 [8, 8192, 16], P('expert', 'tensor'), may hold values from -0.0625 to 0.0625
- down_right: bfloat16 [8, 16, 6144], P('expert', None, 'tensor'), may hold values from -0.29882812 to 0.29882812
Outputs:
- token_grads: bfloat16 [256, 6144], P('expert', 'tensor')
- combine_grads: float32 [256, 2], P('expert')
- gate_first_gradient: float32 [8, 6144, 16], P('expert', 'tensor')
- gate_second_gradient: float32 [8, 16, 8192], P('expert', None, 'tensor')
- upward_first_gradient: float32 [8, 6144, 16], P('expert', 'tensor')
- upward_second_gradient: float32 [8, 16, 8192], P('expert', None, 'tensor')
- down_first_gradient: float32 [8, 8192, 16], P('expert', 'tensor')
- down_second_gradient: float32 [8, 16, 6144], P('expert', None, 'tensor')
The draws below stay inside these ranges and needn't reach their ends.
Inputs may be any that keep to these rules, and one draw needn't show every extreme that they name: `expert_ids`: each token names two different experts. Within each block of 32 consecutive tokens no expert is named by more than 21 tokens, one expert by exactly 21, and every expert by at least one. `slot_pos`: A token's slot for an expert is the number of earlier tokens of its block that name the same expert, so slots of one block and expert are 0, 1, 2 and so on without gaps.
All inputs are finite; a program needn't handle non-finite values.
Results may differ from the reference program's by a relative error of at most 0.024.
Values may be sent and summed in bfloat16 or wider, within the bound.
A program may use at most 64 MiB of HBM per device.

```python
import jax
import jax.numpy as jnp

D = 6144
FF = 8192
EXPERTS = 8
TOPK = 2
RANK = 16
TOK_DEV = 32
CAP = 21
SLOTS = 168
TOKENS = 256


def route_block(block_key):
    key_busy, key_rank, key_extra, key_shuffle, key_swap = jax.random.split(block_key, 5)
    busiest = jax.random.randint(key_busy, (), 0, EXPERTS)
    ranking = jax.random.permutation(key_rank, EXPERTS)
    positions = jnp.arange(EXPERTS, dtype=jnp.int32)
    scores = jnp.where(ranking == busiest, -1, positions)
    sorted_pos = jnp.argsort(scores, stable=True)
    others = ranking[sorted_pos[1:]]
    n_others = EXPERTS - 1
    remaining = 2 * TOK_DEV - CAP
    per_other = max((2 * TOK_DEV - 2 * CAP + n_others - 2) // (n_others - 1), 0)
    cyclic = n_others * per_other
    leftover = remaining - cyclic
    cyclic_labels = others[jnp.arange(cyclic, dtype=jnp.int32) % n_others]
    extra_labels = others[jax.random.randint(key_extra, (leftover,), 0, n_others)]
    labels = jnp.concatenate([jnp.full((CAP,), busiest, jnp.int32), cyclic_labels.astype(jnp.int32), extra_labels.astype(jnp.int32)])
    labels = jnp.sort(labels)
    chosen = jnp.stack([labels[:TOK_DEV], labels[TOK_DEV:]], axis=1)
    shuffle = jax.random.permutation(key_shuffle, TOK_DEV)
    chosen = chosen[shuffle]
    swapped = jax.random.randint(key_swap, (TOK_DEV, 1), 0, 2)
    chosen = jnp.where(swapped == 1, chosen[:, ::-1], chosen)
    onehot = (chosen[:, :, None] == jnp.arange(EXPERTS, dtype=jnp.int32)[None, None, :]).astype(jnp.int32)
    per_token = jnp.sum(onehot, axis=1)
    before = jnp.cumsum(per_token, axis=0) - per_token
    slot_table = jnp.take_along_axis(before, chosen, axis=1)
    return (chosen.astype(jnp.int32), slot_table.astype(jnp.int32))


def route_table(key):
    block_keys = jax.random.split(key, TOKENS // TOK_DEV)
    chosen, slot_table = jax.vmap(route_block)(block_keys)
    return (chosen.reshape(TOKENS, 2), slot_table.reshape(TOKENS, 2))


def draw_expert_ids(key, part):
    chosen, slot_table = route_table(key)
    return chosen


def draw_slot_pos(key, part):
    chosen, slot_table = route_table(key)
    return slot_table


def steps_of(key, dims, cuts, low, largest):
    def one(position, shards_of):
        heights = jax.random.uniform(jax.random.fold_in(jax.random.fold_in(key, 6), position), (shards_of,), jnp.float32, low / len(cuts), largest / len(cuts))
        return jnp.repeat(jnp.exp(heights), dims[position] // shards_of).reshape((-1,) + (1,) * (len(dims) - position - 1))

    gain = one(*cuts[0])
    for cut in cuts[1:]:
        gain = gain * one(*cut)
    return gain


def centred(own_key, extent, spread, limit, cuts=(), held_as=jnp.bfloat16):
    drawn = spread * jax.random.normal(own_key, extent, jnp.float32)
    if cuts:
        drawn = drawn * steps_of(own_key, extent, cuts, -0.22, 0.18)
    return jnp.clip(drawn, -limit, limit).astype(held_as)


def setup_inputs(seed: int = 0) -> dict:
    key_of = jax.random.split(jax.random.key(seed), 15)
    return {
        "tokens": centred(key_of[0], (TOKENS, D), 1.0, 6.0, ((0, 8), (1, 64))),
        "upstream": centred(key_of[1], (TOKENS, D), 0.5, 3.0, ((0, 8), (1, 64))),
        "expert_ids": draw_expert_ids(jax.random.fold_in(key_of[14], 71), 0),
        "slot_pos": draw_slot_pos(jax.random.fold_in(key_of[14], 71), 0),
        "combine": jnp.clip(0.1 + 0.9 * jax.random.uniform(key_of[4], (TOKENS, TOPK), jnp.float32) ** steps_of(key_of[4], (TOKENS, TOPK), ((0, 8),), -0.2, 0.2), 0.1, 1.0),
        "gate_weight": centred(key_of[5], (EXPERTS, D, FF), D ** -0.5, 0.078125, ((0, 8), (2, 64))),
        "upward_weight": centred(key_of[6], (EXPERTS, D, FF), D ** -0.5, 0.078125, ((0, 8), (2, 64))),
        "down_weight": centred(key_of[7], (EXPERTS, FF, D), FF ** -0.5, 0.0625, ((0, 8), (1, 64))),
        "gate_adapter_first": centred(key_of[8], (EXPERTS, D, RANK), D ** -0.5, 0.078125, ((0, 8), (1, 64))),
        "gate_adapter_second": centred(key_of[9], (EXPERTS, RANK, FF), 0.05, 0.29882812, ((0, 8), (2, 64))),
        "upward_adapter_first": centred(key_of[10], (EXPERTS, D, RANK), D ** -0.5, 0.078125, ((0, 8), (1, 64))),
        "upward_adapter_second": centred(key_of[11], (EXPERTS, RANK, FF), 0.05, 0.29882812, ((0, 8), (2, 64))),
        "down_adapter_first": centred(key_of[12], (EXPERTS, FF, RANK), FF ** -0.5, 0.0625, ((0, 8), (1, 64))),
        "down_right": centred(key_of[13], (EXPERTS, RANK, D), 0.05, 0.29882812, ((0, 8), (2, 64))),
    }


adapter_scale_factor = 2.0


def silu_terms(gate_preactivation):
    sigmoid = jax.nn.sigmoid(gate_preactivation)
    active = gate_preactivation * sigmoid
    slope = sigmoid * (1.0 + gate_preactivation * (1.0 - sigmoid))
    return active, slope


def matrix_product(left, right):
    return jnp.dot(left, right, preferred_element_type=jnp.float32)


def reference(tokens, upstream, expert_ids, slot_pos, combine, gate_weight, upward_weight, down_weight, gate_adapter_first, gate_adapter_second, upward_adapter_first, upward_adapter_second, down_adapter_first, down_right):
    block_ids = jnp.arange(TOKENS, dtype=jnp.int32) // TOK_DEV
    row_index = block_ids[:, None] * CAP + slot_pos
    flat_expert = expert_ids.reshape(-1)
    flat_row = row_index.reshape(-1)
    source = jnp.repeat(jnp.arange(TOKENS, dtype=jnp.int32), TOPK)
    slot_x = jnp.zeros((EXPERTS, SLOTS, D), jnp.float32).at[flat_expert, flat_row].set(tokens[source].astype(jnp.float32)).astype(jnp.bfloat16)
    slot_g = jnp.zeros((EXPERTS, SLOTS, D), jnp.float32).at[flat_expert, flat_row].set(upstream[source].astype(jnp.float32)).astype(jnp.bfloat16)
    slot_c = jnp.zeros((EXPERTS, SLOTS), jnp.float32).at[flat_expert, flat_row].set(combine.reshape(-1))
    output_rows = [[], [], [], [], [], [], [], []]
    for expert_index in range(EXPERTS):
        input_rows = slot_x[expert_index]
        gradient_list = slot_g[expert_index]
        weight_col = slot_c[expert_index][:, None]
        gate_reduced = matrix_product(input_rows, gate_adapter_first[expert_index]).astype(jnp.bfloat16)
        upward_reduced = matrix_product(input_rows, upward_adapter_first[expert_index]).astype(jnp.bfloat16)
        down_reduced = matrix_product(gradient_list, down_right[expert_index].T)
        gate_preactivation = matrix_product(input_rows, gate_weight[expert_index]) + adapter_scale_factor * matrix_product(gate_reduced, gate_adapter_second[expert_index])
        upward_preactivation = matrix_product(input_rows, upward_weight[expert_index]) + adapter_scale_factor * matrix_product(upward_reduced, upward_adapter_second[expert_index])
        active, slope = silu_terms(gate_preactivation)
        hidden_state = (active * upward_preactivation).astype(jnp.bfloat16)
        hidden_backward = matrix_product(gradient_list, down_weight[expert_index].T) + adapter_scale_factor * matrix_product(down_reduced.astype(jnp.bfloat16), down_adapter_first[expert_index].T)
        slot_grads = jnp.sum(hidden_state.astype(jnp.float32) * hidden_backward, axis=1)
        grad_hidden = weight_col * hidden_backward
        gate_gradient = (grad_hidden * upward_preactivation * slope).astype(jnp.bfloat16)
        upward_gradient = (grad_hidden * active).astype(jnp.bfloat16)
        reduced_weighted = (weight_col * matrix_product(hidden_state, down_adapter_first[expert_index])).astype(jnp.bfloat16)
        down_weighted = (weight_col * down_reduced).astype(jnp.bfloat16)
        gate_backward = matrix_product(gate_gradient, gate_adapter_second[expert_index].T).astype(jnp.bfloat16)
        upward_backward = matrix_product(upward_gradient, upward_adapter_second[expert_index].T).astype(jnp.bfloat16)
        output_rows[0].append(adapter_scale_factor * matrix_product(input_rows.T, gate_backward))
        output_rows[1].append(adapter_scale_factor * matrix_product(gate_reduced.T, gate_gradient))
        output_rows[2].append(adapter_scale_factor * matrix_product(input_rows.T, upward_backward))
        output_rows[3].append(adapter_scale_factor * matrix_product(upward_reduced.T, upward_gradient))
        output_rows[4].append(adapter_scale_factor * matrix_product(hidden_state.T, down_weighted))
        output_rows[5].append(adapter_scale_factor * matrix_product(reduced_weighted.T, gradient_list))
        slot_input_rows = matrix_product(gate_gradient, gate_weight[expert_index].T) + matrix_product(upward_gradient, upward_weight[expert_index].T)
        slot_input_rows = slot_input_rows + adapter_scale_factor * (matrix_product(gate_backward, gate_adapter_first[expert_index].T) + matrix_product(upward_backward, upward_adapter_first[expert_index].T))
        output_rows[6].append(slot_input_rows)
        output_rows[7].append(slot_grads)
    slot_inputs = jnp.stack(output_rows[6])
    slot_grads_all = jnp.stack(output_rows[7])
    first = slot_inputs[expert_ids[:, 0], row_index[:, 0]]
    second = slot_inputs[expert_ids[:, 1], row_index[:, 1]]
    token_grads = (first + second).astype(jnp.bfloat16)
    combine_grads = slot_grads_all[expert_ids, row_index]
    return (token_grads, combine_grads, jnp.stack(output_rows[0]), jnp.stack(output_rows[1]), jnp.stack(output_rows[2]), jnp.stack(output_rows[3]), jnp.stack(output_rows[4]), jnp.stack(output_rows[5]))
```

```python
import jax
import jax.numpy as jnp
from jax import lax
from jax.experimental import pallas as pl
from jax.experimental.pallas import tpu as pltpu
from jax.sharding import PartitionSpec as P

MESH = pl.DeviceIdType.MESH
F32 = jnp.float32
BF16 = jnp.bfloat16
SCALE = 2.0
NX, NY, NZ, NC = 4, 4, 16, 2
TB = 32
FD = 96
HR = 48
HID = 128
NT = 256
STEP = 4 * FD
PAIR = 2


def dot_nn(a, b):
    return lax.dot_general(a, b, (((1,), (0,)), ((), ())), preferred_element_type=F32)


def dot_nt(a, b):
    return lax.dot_general(a, b, (((1,), (1,)), ((), ())), preferred_element_type=F32)


def dot_tn(a, b):
    return lax.dot_general(a, b, (((0,), (0,)), ((), ())), preferred_element_type=F32)


def remote(src, dst, send, recv, dev):
    return pltpu.make_async_remote_copy(
        src_ref=src, dst_ref=dst, send_sem=send, recv_sem=recv, device_id=dev, device_id_type=MESH
    )


def loop(low, high, body):
    def step(i, carry):
        body(i)
        return carry

    lax.fori_loop(low, high, step, 0)


def kernel(
    tok,
    ups,
    ids,
    comb,
    w1_hbm,
    w3_hbm,
    w2_hbm,
    a1t,
    b1,
    a3t,
    b3,
    d1t,
    rj,
    tg,
    cg,
    gft,
    gs,
    uft,
    us,
    dft,
    ds,
    w1,
    w3,
    w2,
    w13t,
    src,
    disp,
    xj,
    gj,
    own,
    gat,
    acch,
    accq,
    et,
    part,
    rsb,
    ysend,
    yrec,
    full,
    yb,
    rc,
    axb,
    byb,
    ya,
    yc,
    ayb,
    bxb,
    zsend,
    zr,
    fscr,
    fsend,
    fin,
    ascr,
    asend,
    afin,
    w_sem,
    d_ss,
    d_rs,
    z_ss,
    z_rs,
    a1_ss,
    a1_rs,
    b1_ss,
    b1_rs,
    a2_ss,
    a2_rs,
    b2_ss,
    b2_rs,
    s1_ss,
    s1_rs,
    s2_ss,
    s2_rs,
    r_ss,
    r_rs,
    y_ss,
    y_rs,
    g_ss,
    g_rs,
    k_ss,
    k_rs,
    p1_ss,
    p1_rs,
    p2_ss,
    p2_rs,
    p3_ss,
    p3_rs,
    f_ss,
    f_rs,
    h_ss,
    h_rs,
):
    e = lax.axis_index("expert")
    j = lax.axis_index("tensor")
    x = e // 2
    c = lax.rem(e, 2)
    y = j // NZ
    z = lax.rem(j, NZ)
    sib = (2 * x + 1 - c, j)

    def at_x(v):
        return (2 * v + c, j)

    def at_y(v):
        return (e, v * NZ + z)

    def at_z(v):
        return (e, y * NZ + v)

    bar = pltpu.get_barrier_semaphore()

    def sig_e(i):
        pl.semaphore_signal(bar, inc=1, device_id=(lax.rem(e + i, 8), j), device_id_type=MESH)

    def sig_z(i):
        pl.semaphore_signal(bar, inc=1, device_id=at_z(lax.rem(z + i, NZ)), device_id_type=MESH)

    def sig_y(i):
        pl.semaphore_signal(bar, inc=1, device_id=at_y(lax.rem(y + i, NY)), device_id_type=MESH)

    loop(1, NZ, sig_z)
    loop(1, NY, sig_y)
    loop(1, 8, sig_e)

    loads = [
        pltpu.make_async_copy(w1_hbm.at[0], w1, w_sem.at[0]),
        pltpu.make_async_copy(w3_hbm.at[0], w3, w_sem.at[1]),
        pltpu.make_async_copy(w2_hbm.at[0], w2, w_sem.at[2]),
    ]
    for load in loads:
        load.start()

    lane = lax.broadcasted_iota(jnp.int32, (TB, 128), 1)
    idv = ids[...]
    cv = comb[...]
    dense = jnp.zeros((TB, 128), F32)
    for k in range(2):
        hit = (lane - FD == idv[:, k : k + 1]) | (lane - FD - 8 == idv[:, k : k + 1])
        dense = dense + jnp.where(hit, cv[:, k : k + 1], 0.0)
    high = dense.astype(BF16)
    low = (dense - high.astype(F32)).astype(BF16)
    src[0:TB, :] = jnp.where(lane < FD + 8, high.astype(F32), low.astype(F32)).astype(BF16)
    src[0:TB, 0:FD] = tok[...]
    src[TB : 2 * TB, :] = jnp.zeros((TB, 128), BF16)
    src[TB : 2 * TB, 0:FD] = ups[...]
    disp[e] = src[...]

    for load in loads:
        load.wait()

    def flip(i):
        rows = pl.ds(pl.multiple_of(i * 128, 128), 128)
        w13t[0:HID, rows] = jnp.transpose(w1[rows, :])
        w13t[HID : 2 * HID, rows] = jnp.transpose(w3[rows, :])

    loop(0, 48, flip)

    pl.semaphore_wait(bar, 7 + NZ - 1 + NY - 1)

    def disp_copy(i, slot):
        return remote(
            src, disp.at[slot], d_ss.at[i], d_rs.at[i], (lax.rem(e + i, 8), j)
        )

    loop(1, 8, lambda i: disp_copy(i, e).start())
    loop(1, 8, lambda i: disp_copy(i, lax.rem(e + 8 - i, 8)).wait())

    xt = jnp.transpose(disp[:, 0:TB, :].reshape(NT, 128))
    gt = jnp.transpose(disp[:, TB : 2 * TB, :].reshape(NT, 128))
    row = lax.broadcasted_iota(jnp.int32, (32, NT), 0)
    tail = xt[FD:128, :].astype(F32)
    weight = jnp.sum(jnp.where((row == e) | (row == e + 8), tail, 0.0), axis=0, keepdims=True)
    xj[...] = xt[0:FD, :]
    gj[...] = gt[0:FD, :]
    for half in range(2):
        for th in range(2):
            cut = slice(128 * th, 128 * th + 128)
            rows = slice(HR * half, HR * half + HR)
            own[th, half] = xt[rows, cut]
            own[2 + th, half] = gt[rows, cut]
    gat[x, y, z, c] = own[x, c]

    def z_copy(i, slot):
        piece = gat.at[x, y, slot, c]
        return remote(piece, piece, z_ss.at[i], z_rs.at[i], at_z(lax.rem(z + i, NZ)))

    loop(1, NZ, lambda i: z_copy(i, z).start())

    def sum_start(n, value):
        for k in range(NZ):
            part[n, k] = value[8 * (k // 2) : 8 * (k // 2) + 8, 128 * (k % 2) : 128 * (k % 2) + 128]
        rsb[n, z] = part[n, z]

        def go(i):
            to = lax.rem(z + i, NZ)
            remote(part.at[n, to], rsb.at[n, z], r_ss.at[n, i], r_rs.at[n, i], at_z(to)).start()

        loop(1, NZ, go)

    def y_copy(n, i, slot):
        return remote(
            ysend.at[n], yrec.at[n, slot], y_ss.at[n, i], y_rs.at[n, i], at_y(lax.rem(y + i, NY))
        )

    def sum_middle(n):
        def done(i):
            to = lax.rem(z + i, NZ)
            remote(
                part.at[n, to],
                rsb.at[n, lax.rem(z + NZ - i, NZ)],
                r_ss.at[n, i],
                r_rs.at[n, i],
                at_z(to),
            ).wait()

        loop(1, NZ, done)
        total = jnp.sum(rsb[n], axis=0)
        ysend[n] = total
        yrec[n, y] = total
        loop(1, NY, lambda i: y_copy(n, i, y).start())

    def g_copy(n, i, slot):
        piece = full.at[n, slot]
        return remote(piece, piece, g_ss.at[n, i], g_rs.at[n, i], at_z(lax.rem(z + i, NZ)))

    def sum_last(n):
        loop(1, NY, lambda i: y_copy(n, i, lax.rem(y + NY - i, NY)).wait())
        full[n, z] = jnp.sum(yrec[n], axis=0)
        loop(1, NZ, lambda i: g_copy(n, i, z).start())

    def sum_done(n):
        loop(1, NZ, lambda i: g_copy(n, i, lax.rem(z + NZ - i, NZ)).wait())
        return jnp.concatenate(
            [jnp.concatenate([full[n, 2 * k], full[n, 2 * k + 1]], axis=1) for k in range(8)], axis=0
        )

    a13t = jnp.concatenate([a1t[0], a3t[0]], axis=0)
    sum_start(
        0,
        jnp.concatenate(
            [dot_nn(a13t, xj[...]), dot_nn(rj[0], gj[...]), jnp.zeros((16, NT), F32)], axis=0
        ),
    )

    loop(1, NZ, lambda i: z_copy(i, lax.rem(z + NZ - i, NZ)).wait())
    sum_middle(0)

    ahead_x = lax.rem(x + 1 + 2 * c, NX)
    behind_x = lax.rem(x + 3 + 2 * c, NX)
    far_x = lax.rem(x + 2, NX)
    ahead_y = lax.rem(y + 1 + 2 * c, NY)
    behind_y = lax.rem(y + 3 + 2 * c, NY)
    far_y = lax.rem(y + 2, NY)

    def a1_copy(k, of, to):
        piece = gat.at[of, y, 0:8, c]
        return remote(piece, piece, a1_ss.at[k], a1_rs.at[k], at_x(to))

    def b1_copy(k, of, to):
        piece = gat.at[x, of, 8:16, c]
        return remote(piece, piece, b1_ss.at[k], b1_rs.at[k], at_y(to))

    a1_copy(0, x, ahead_x).start()
    b1_copy(0, y, ahead_y).start()
    a1_copy(1, x, behind_x).start()
    b1_copy(1, y, behind_y).start()
    a1_copy(0, behind_x, ahead_x).wait_recv()
    a1_copy(2, behind_x, ahead_x).start()
    b1_copy(0, behind_y, ahead_y).wait_recv()
    b1_copy(2, behind_y, ahead_y).start()
    a1_copy(1, ahead_x, behind_x).wait_recv()
    b1_copy(1, ahead_y, behind_y).wait_recv()
    sum_last(0)
    a1_copy(2, far_x, ahead_x).wait_recv()
    b1_copy(2, far_y, ahead_y).wait_recv()

    def a2_copy(k, i, of, to):
        piece = gat.at[:, of, pl.ds(PAIR * i, PAIR), c]
        return remote(piece, piece, a2_ss.at[k, i], a2_rs.at[k, i], at_y(to))

    def b2_copy(k, i, of, to):
        piece = gat.at[of, :, pl.ds(8 + PAIR * i, PAIR), c]
        return remote(piece, piece, b2_ss.at[k, i], b2_rs.at[k, i], at_x(to))

    def sa_copy(k, i, of, core):
        piece = gat.at[:, of, pl.ds(PAIR * i, PAIR), core]
        return remote(piece, piece, s1_ss.at[k, i], s1_rs.at[k, i], sib)

    def sb_copy(k, i, of, core):
        piece = gat.at[of, :, pl.ds(8 + PAIR * i, PAIR), core]
        return remote(piece, piece, s2_ss.at[k, i], s2_rs.at[k, i], sib)

    chunks = 8 // PAIR

    def wide_start(i):
        a2_copy(0, i, y, ahead_y).start()
        b2_copy(0, i, x, ahead_x).start()
        a2_copy(1, i, y, behind_y).start()
        b2_copy(1, i, x, behind_x).start()
        sa_copy(0, i, y, c).start()
        sb_copy(0, i, x, c).start()

    loop(0, chunks, wide_start)

    def wide_pass(i):
        a2_copy(0, i, behind_y, ahead_y).wait_recv()
        a2_copy(2, i, behind_y, ahead_y).start()
        sa_copy(1, i, behind_y, c).start()
        b2_copy(0, i, behind_x, ahead_x).wait_recv()
        b2_copy(2, i, behind_x, ahead_x).start()
        sb_copy(1, i, behind_x, c).start()
        a2_copy(1, i, ahead_y, behind_y).wait_recv()
        sa_copy(2, i, ahead_y, c).start()
        b2_copy(1, i, ahead_x, behind_x).wait_recv()
        sb_copy(2, i, ahead_x, c).start()

    loop(0, chunks, wide_pass)

    def wide_end(i):
        a2_copy(2, i, far_y, ahead_y).wait_recv()
        sa_copy(3, i, far_y, c).start()
        b2_copy(2, i, far_x, ahead_x).wait_recv()
        sb_copy(3, i, far_x, c).start()

    loop(0, chunks, wide_end)

    def sib_end(i):
        sa_copy(0, i, y, 1 - c).wait()
        sb_copy(0, i, x, 1 - c).wait()
        sa_copy(1, i, ahead_y, 1 - c).wait()
        sb_copy(1, i, ahead_x, 1 - c).wait()
        sa_copy(2, i, behind_y, 1 - c).wait()
        sb_copy(2, i, behind_x, 1 - c).wait()
        sa_copy(3, i, far_y, 1 - c).wait()
        sb_copy(3, i, far_x, 1 - c).wait()

    loop(0, chunks, sib_end)

    acch[...] = jnp.zeros_like(acch)
    accq[...] = jnp.zeros_like(accq)

    def project(i):
        zs = pl.ds(4 * lax.rem(i, 4), 4)
        cols = pl.ds(pl.multiple_of(i * STEP, 128), STEP)

        def side(n):
            return gat[n, i // 4, zs].reshape(STEP, 128)

        acch[...] += dot_nn(w13t[:, cols], jnp.concatenate([side(0), side(1)], axis=1))
        accq[...] += dot_nn(w2[:, cols], jnp.concatenate([side(2), side(3)], axis=1))

    loop(0, 16, project)

    low_sums = sum_done(0)
    u1 = low_sums[0:16].astype(BF16)
    u3 = low_sums[16:32].astype(BF16)
    v = low_sums[32:48]
    h1 = acch[0:HID] + SCALE * dot_tn(b1[0], u1)
    h3 = acch[HID : 2 * HID] + SCALE * dot_tn(b3[0], u3)
    q = accq[...] + SCALE * dot_tn(d1t[0], v.astype(BF16))
    sig = jax.nn.sigmoid(h1)
    active = h1 * sig
    slope = sig * (1.0 + h1 * (1.0 - sig))
    hidden = (active * h3).astype(BF16)
    back = weight * q
    e1 = (back * h3 * slope).astype(BF16)
    e3 = (back * active).astype(BF16)
    kk = jnp.sum(hidden.astype(F32) * q, axis=0, keepdims=True)
    et[0:HID, :] = e1
    et[HID : 2 * HID, :] = e3
    sum_start(
        1,
        jnp.concatenate(
            [
                dot_nn(b1[0], e1),
                dot_nn(b3[0], e3),
                dot_nn(d1t[0], hidden),
                kk,
                jnp.zeros((15, NT), F32),
            ],
            axis=0,
        ),
    )

    def grads(i, zoff):
        yy = i // 2
        zz = zoff + 4 * lax.rem(i, 2)
        rows = pl.ds(pl.multiple_of((yy * NZ + zz) * FD, FD), STEP)
        wide = jnp.concatenate([w1[rows, :], w3[rows, :]], axis=1)
        out = dot_nn(wide, et[...]).astype(BF16).reshape(4, 2, HR, NT)
        for rh in range(2):
            for th in range(2):
                yb[2 * rh + th, yy, pl.ds(zz, 4)] = out[:, rh, :, 128 * th : 128 * th + 128]

    mine = 8 * c
    other = 8 - mine
    loop(0, 8, lambda i: grads(i, other))

    def k_copy():
        return remote(yb.at[:, :, pl.ds(other, 8)], rc, k_ss.at[0], k_rs.at[0], sib)

    k_copy().start()
    loop(0, 8, lambda i: grads(i, mine))

    dft[0] = SCALE * dot_nt((weight * v).astype(BF16), hidden)
    gs[0] = SCALE * dot_nt(u1, e1)
    us[0] = SCALE * dot_nt(u3, e3)

    k_copy().wait()

    def add_core(i):
        xx = i // 4
        yy = lax.rem(i, 4)
        both = yb[xx, yy, pl.ds(mine, 8)].astype(F32) + rc[xx, yy].astype(F32)
        yb[xx, yy, pl.ds(mine, 8)] = both.astype(BF16)

    loop(0, 16, add_core)

    def px_copy(i):
        to = lax.rem(x + i, NX)
        return remote(
            yb.at[to, :, pl.ds(mine, 4)], axb.at[i], p1_ss.at[0, i], p1_rs.at[0, i], at_x(to)
        )

    def py_copy(i):
        to = lax.rem(y + i, NY)
        return remote(
            yb.at[:, to, pl.ds(mine + 4, 4)], byb.at[i], p1_ss.at[1, i], p1_rs.at[1, i], at_y(to)
        )

    for i in (1, 3, 2):
        px_copy(i).start()
        py_copy(i).start()

    sum_middle(1)

    for i in (1, 3, 2):
        px_copy(i).wait()
        py_copy(i).wait()

    def add_first(i):
        sa = yb[x, i, pl.ds(mine, 4)].astype(F32)
        sb = yb[i, y, pl.ds(mine + 4, 4)].astype(F32)
        for k in (1, 2, 3):
            sa = sa + axb[k, i].astype(F32)
            sb = sb + byb[k, i].astype(F32)
        ya[i] = sa.astype(BF16)
        yc[i] = sb.astype(BF16)

    loop(0, 4, add_first)

    def qy_copy(i):
        to = lax.rem(y + i, NY)
        return remote(ya.at[to], ayb.at[i], p2_ss.at[0, i], p2_rs.at[0, i], at_y(to))

    def qx_copy(i):
        to = lax.rem(x + i, NX)
        return remote(yc.at[to], bxb.at[i], p2_ss.at[1, i], p2_rs.at[1, i], at_x(to))

    for i in (1, 3, 2):
        qy_copy(i).start()
        qx_copy(i).start()

    sum_last(1)

    for i in (1, 3, 2):
        qy_copy(i).wait()
        qx_copy(i).wait()

    sa = ya[y].astype(F32)
    sb = yc[x].astype(F32)
    for k in (1, 2, 3):
        sa = sa + ayb[k].astype(F32)
        sb = sb + bxb[k].astype(F32)
    zsend[0:4] = sa.astype(BF16)
    zsend[4:8] = sb.astype(BF16)

    holder = z // 8 == c

    def t_copy(k, i, slot):
        return remote(
            zsend.at[k], zr.at[slot], p3_ss.at[k], p3_rs.at[i], at_z(mine + k)
        )

    def t_start(k):
        to = mine + k

        @pl.when(to != z)
        def _():
            t_copy(k, lax.rem(to + NZ - z, NZ), z).start()

    loop(0, 8, t_start)

    sums = sum_done(1)
    r13 = sums[0:32].astype(BF16)
    zt = (weight * sums[32:48]).astype(BF16)
    first = SCALE * dot_nt(r13, xj[...])
    gft[0] = first[0:16]
    uft[0] = first[16:32]
    ds[0] = SCALE * dot_nt(zt, gj[...])
    ascr[FD:128, :] = jnp.zeros((128 - FD, NT), F32)
    ascr[0:FD, :] = SCALE * dot_tn(a13t, r13)
    ascr[FD : FD + 1, :] = sums[48:49]
    asend[...] = jnp.transpose(ascr[...]).astype(BF16).reshape(8, TB, 128)
    afin[e] = asend[e]

    def h_copy(i, slot):
        to = lax.rem(e + i, 8)
        return remote(asend.at[to], afin.at[slot], h_ss.at[i], h_rs.at[i], (to, j))

    loop(1, 8, lambda i: h_copy(i, e).start())

    def t_sent(k):
        @pl.when(mine + k != z)
        def _():
            t_copy(k, 0, z).wait_send()

    loop(0, 8, t_sent)

    rh = x // 2
    th = lax.rem(x, 2)

    def f_copy(i):
        return remote(fsend.at[i], fin.at[rh], f_ss.at[i], f_rs.at[rh], (4 * th + i, j))

    @pl.when(holder)
    def _():
        zr[z] = zsend[lax.rem(z, 8)]

        def got(i):
            t_copy(0, i, lax.rem(z + NZ - i, NZ)).wait_recv()

        loop(1, NZ, got)
        fscr[...] = jnp.zeros_like(fscr)
        fscr[pl.ds(pl.multiple_of(HR * rh, HR), HR), :] = jnp.sum(zr[...].astype(F32), axis=0)
        fsend[...] = jnp.transpose(fscr[...]).astype(BF16).reshape(4, TB, 128)
        for i in range(4):

            @pl.when(4 * th + i == e)
            def _():
                fin[rh] = fsend[i]

            @pl.when(4 * th + i != e)
            def _():
                f_copy(i).start()

    loop(1, 8, lambda i: h_copy(i, lax.rem(e + 8 - i, 8)).wait())

    total = jnp.zeros((TB, 128), F32)
    first_k = jnp.zeros((TB, 1), F32)
    second_k = jnp.zeros((TB, 1), F32)
    for n in range(8):
        block = afin[n].astype(F32)
        total = total + block
        column = block[:, FD : FD + 1]
        first_k = first_k + jnp.where(idv[:, 0:1] == n, column, 0.0)
        second_k = second_k + jnp.where(idv[:, 1:2] == n, column, 0.0)
    cg[:, 0:1] = first_k
    cg[:, 1:2] = second_k

    for n in range(2):

        @pl.when(4 * n + 2 * (e // 4) + z // 8 != e)
        def _():
            remote(fsend.at[0], fin.at[n], f_ss.at[0], f_rs.at[n], (e, j)).wait_recv()

    total = total + fin[0].astype(F32) + fin[1].astype(F32)
    tg[...] = total[:, 0:FD].astype(BF16)

    @pl.when(holder)
    def _():
        for i in range(4):

            @pl.when(4 * th + i != e)
            def _():
                f_copy(i).wait_send()

    for k in range(3):
        a1_copy(k, x, ahead_x).wait_send()
        b1_copy(k, y, ahead_y).wait_send()

        def sent(i):
            a2_copy(k, i, y, ahead_y).wait_send()
            b2_copy(k, i, x, ahead_x).wait_send()

        loop(0, chunks, sent)


def local(
    tokens,
    upstream,
    expert_ids,
    slot_pos,
    combine,
    gate_weight,
    upward_weight,
    down_weight,
    gate_adapter_first,
    gate_adapter_second,
    upward_adapter_first,
    upward_adapter_second,
    down_adapter_first,
    down_right,
):
    vmem = pl.BlockSpec(memory_space=pltpu.VMEM)
    hbm = pl.BlockSpec(memory_space=pl.ANY)
    dma = pltpu.SemaphoreType.DMA

    def buf(shape, dtype=BF16):
        return pltpu.VMEM(shape, dtype)

    chunks = 8 // PAIR
    outs = pl.pallas_call(
        kernel,
        out_shape=(
            jax.ShapeDtypeStruct((TB, FD), BF16),
            jax.ShapeDtypeStruct((TB, 2), F32),
            jax.ShapeDtypeStruct((1, 16, FD), F32),
            jax.ShapeDtypeStruct((1, 16, HID), F32),
            jax.ShapeDtypeStruct((1, 16, FD), F32),
            jax.ShapeDtypeStruct((1, 16, HID), F32),
            jax.ShapeDtypeStruct((1, 16, HID), F32),
            jax.ShapeDtypeStruct((1, 16, FD), F32),
        ),
        in_specs=[vmem] * 4 + [hbm] * 3 + [vmem] * 6,
        out_specs=[vmem] * 8,
        scratch_shapes=[
            buf((6144, HID)),
            buf((6144, HID)),
            buf((HID, 6144)),
            buf((2 * HID, 6144)),
            buf((2 * TB, 128)),
            buf((8, 2 * TB, 128)),
            buf((FD, NT)),
            buf((FD, NT)),
            buf((NX, NC, HR, 128)),
            buf((NX, NY, NZ, NC, HR, 128)),
            buf((2 * HID, NT), F32),
            buf((HID, NT), F32),
            buf((2 * HID, NT)),
            buf((2, NZ, 8, 128), F32),
            buf((2, NZ, 8, 128), F32),
            buf((2, 8, 128), F32),
            buf((2, NY, 8, 128), F32),
            buf((2, NZ, 8, 128), F32),
            buf((NX, NY, NZ, HR, 128)),
            buf((NX, NY, 8, HR, 128)),
            buf((4, NY, 4, HR, 128)),
            buf((4, NX, 4, HR, 128)),
            buf((NY, 4, HR, 128)),
            buf((NX, 4, HR, 128)),
            buf((4, 4, HR, 128)),
            buf((4, 4, HR, 128)),
            buf((8, HR, 128)),
            buf((NZ, HR, 128)),
            buf((128, 128), F32),
            buf((4, TB, 128)),
            buf((2, TB, 128)),
            buf((128, NT), F32),
            buf((8, TB, 128)),
            buf((8, TB, 128)),
            dma((3,)),
            dma((8,)),
            dma((8,)),
            dma((NZ,)),
            dma((NZ,)),
            dma((3,)),
            dma((3,)),
            dma((3,)),
            dma((3,)),
            dma((3, chunks)),
            dma((3, chunks)),
            dma((3, chunks)),
            dma((3, chunks)),
            dma((4, chunks)),
            dma((4, chunks)),
            dma((4, chunks)),
            dma((4, chunks)),
            dma((2, NZ)),
            dma((2, NZ)),
            dma((2, NY)),
            dma((2, NY)),
            dma((2, NZ)),
            dma((2, NZ)),
            dma((1,)),
            dma((1,)),
            dma((2, 4)),
            dma((2, 4)),
            dma((2, 4)),
            dma((2, 4)),
            dma((8,)),
            dma((NZ,)),
            dma((4,)),
            dma((2,)),
            dma((8,)),
            dma((8,)),
        ],
        compiler_params=pltpu.CompilerParams(
            collective_id=0, has_side_effects=True, vmem_limit_bytes=48 * 2**20
        ),
        name="moe_backward",
    )(
        tokens,
        upstream,
        expert_ids,
        combine,
        gate_weight,
        upward_weight,
        down_weight,
        jnp.swapaxes(gate_adapter_first, 1, 2),
        gate_adapter_second,
        jnp.swapaxes(upward_adapter_first, 1, 2),
        upward_adapter_second,
        jnp.swapaxes(down_adapter_first, 1, 2),
        down_right,
    )
    token_grads, combine_grads, gft, gs, uft, us, dft, ds = outs
    return (
        token_grads,
        combine_grads,
        jnp.swapaxes(gft, 1, 2),
        gs,
        jnp.swapaxes(uft, 1, 2),
        us,
        jnp.swapaxes(dft, 1, 2),
        ds,
    )


def solution(mesh):
    in_specs = (
        P("expert", "tensor"),
        P("expert", "tensor"),
        P("expert", None),
        P("expert", None),
        P("expert", None),
        P("expert", None, "tensor"),
        P("expert", None, "tensor"),
        P("expert", "tensor", None),
        P("expert", "tensor", None),
        P("expert", None, "tensor"),
        P("expert", "tensor", None),
        P("expert", None, "tensor"),
        P("expert", "tensor", None),
        P("expert", None, "tensor"),
    )
    out_specs = (
        P("expert", "tensor"),
        P("expert", None),
        P("expert", "tensor", None),
        P("expert", None, "tensor"),
        P("expert", "tensor", None),
        P("expert", None, "tensor"),
        P("expert", "tensor", None),
        P("expert", None, "tensor"),
    )
    return jax.shard_map(local, mesh=mesh, in_specs=in_specs, out_specs=out_specs, check_vma=False)
```

```python
import jax
import jax.numpy as jnp
from jax import lax
from jax.experimental import pallas as pl
from jax.experimental.pallas import tpu as pltpu
from jax.sharding import PartitionSpec as P

MESH = pl.DeviceIdType.MESH
F32 = jnp.float32
BF16 = jnp.bfloat16
SCALE = 2.0
NX, NY, NZ, NC = 4, 4, 16, 2
TB = 32
FD = 96
HR = 48
HID = 128
NT = 256
STEP = 4 * FD
GRANT = 60 * 2**20
NEAR = 4


def dot_nn(a, b):
    return lax.dot_general(a, b, (((1,), (0,)), ((), ())), preferred_element_type=F32)


def dot_nt(a, b):
    return lax.dot_general(a, b, (((1,), (1,)), ((), ())), preferred_element_type=F32)


def dot_tn(a, b):
    return lax.dot_general(a, b, (((0,), (0,)), ((), ())), preferred_element_type=F32)


def remote(src, dst, send, recv, dev):
    return pltpu.make_async_remote_copy(
        src_ref=src, dst_ref=dst, send_sem=send, recv_sem=recv, device_id=dev, device_id_type=MESH
    )


def loop(low, high, body):
    def step(i, carry):
        body(i)
        return carry

    lax.fori_loop(low, high, step, 0)


def kernel(
    tok_hbm,
    ups_hbm,
    ids_hbm,
    comb_hbm,
    w1_hbm,
    w3_hbm,
    w2_hbm,
    a1t_hbm,
    b1_hbm,
    a3t_hbm,
    b3_hbm,
    d1t_hbm,
    rj_hbm,
    tg,
    cg,
    gft,
    gs,
    uft,
    us,
    dft,
    ds,
    tok,
    ups,
    ids,
    comb,
    a1t,
    b1,
    a3t,
    b3,
    d1t,
    rj,
    w1,
    w3,
    w2,
    w13t,
    wide_t,
    src,
    disp,
    xj,
    gj,
    own,
    gat,
    acch,
    accq,
    et,
    part,
    rsb,
    ysend,
    yrec,
    full,
    yb,
    rc,
    axo,
    byo,
    axr,
    byr,
    ya,
    yc,
    ayb,
    bxb,
    zsend,
    zr,
    fscr,
    fsend,
    fin,
    ascr,
    asend,
    afin,
    w_sem,
    d_ss,
    d_rs,
    z_ss,
    z_rs,
    a1_ss,
    a1_rs,
    b1_ss,
    b1_rs,
    a2_ss,
    a2_rs,
    b2_ss,
    b2_rs,
    s1_ss,
    s1_rs,
    s2_ss,
    s2_rs,
    r_ss,
    r_rs,
    y_ss,
    y_rs,
    g_ss,
    g_rs,
    k_ss,
    k_rs,
    p1_ss,
    p1_rs,
    p2_ss,
    p2_rs,
    p3_ss,
    p3_rs,
    f_ss,
    f_rs,
    h_ss,
    h_rs,
    known,
):
    e = lax.axis_index("expert")
    j = lax.axis_index("tensor")
    x = e // 2
    c = lax.rem(e, 2)
    y = j // NZ
    z = lax.rem(j, NZ)
    sib = (2 * x + 1 - c, j)

    def at_x(v):
        return (2 * v + c, j)

    def at_y(v):
        return (e, v * NZ + z)

    def at_z(v):
        return (e, y * NZ + v)

    bar = pltpu.get_barrier_semaphore()

    def sig_e(i):
        pl.semaphore_signal(bar, inc=1, device_id=(lax.rem(e + i, 8), j), device_id_type=MESH)

    def sig_z(i):
        pl.semaphore_signal(bar, inc=1, device_id=at_z(lax.rem(z + i, NZ)), device_id_type=MESH)

    def sig_y(i):
        pl.semaphore_signal(bar, inc=1, device_id=at_y(lax.rem(y + i, NY)), device_id_type=MESH)

    loop(1, NEAR + 1, sig_z)
    loop(NZ - NEAR, NZ, sig_z)
    loop(1, NY, sig_y)
    loop(1, 8, sig_e)

    pairs = [
        (tok_hbm, tok),
        (ups_hbm, ups),
        (ids_hbm, ids),
        (comb_hbm, comb),
        (a1t_hbm, a1t),
        (b1_hbm, b1),
        (a3t_hbm, a3t),
        (b3_hbm, b3),
        (d1t_hbm, d1t),
        (rj_hbm, rj),
        (w1_hbm.at[0], w1),
        (w3_hbm.at[0], w3),
        (w2_hbm.at[0], w2),
    ]
    loads = [pltpu.make_async_copy(a, b, w_sem.at[n]) for n, (a, b) in enumerate(pairs)]
    for load in loads:
        load.start()
    for load in loads[0:4]:
        load.wait()

    expert_row = lax.broadcasted_iota(jnp.int32, (8, TB), 0)
    dense = jnp.zeros((8, TB), F32)
    for k in range(2):
        dense = dense + jnp.where(expert_row == ids[k : k + 1, :], comb[k : k + 1, :], 0.0)
    high = dense.astype(BF16).astype(F32)
    wide_t[...] = jnp.zeros_like(wide_t)
    wide_t[0:2, 0:TB] = ids[...].astype(F32)
    wide_t[FD : FD + 8, 0:TB] = high
    wide_t[FD + 8 : FD + 16, 0:TB] = dense - high
    wide = jnp.transpose(wide_t[...])[0:TB, :]
    id0 = wide[:, 0:1]
    id1 = wide[:, 1:2]
    src[0:TB, :] = wide.astype(BF16)
    src[0:TB, 0:FD] = tok[...]
    src[TB : 2 * TB, :] = jnp.zeros((TB, 128), BF16)
    src[TB : 2 * TB, 0:FD] = ups[...]
    disp[e] = src[...]
    for load in loads[4:]:
        load.wait()

    def flip(i):
        rows = pl.ds(pl.multiple_of(i * 128, 128), 128)
        w13t[0:HID, rows] = jnp.transpose(w1[rows, :])
        w13t[HID : 2 * HID, rows] = jnp.transpose(w3[rows, :])


    pl.semaphore_wait(bar, 7 + 2 * NEAR + NY - 1)

    def disp_copy(i, slot):
        return remote(
            src, disp.at[slot], d_ss.at[i], d_rs.at[i], (lax.rem(e + i, 8), j)
        )

    loop(1, 8, lambda i: disp_copy(i, e).start())
    for step in (NEAR, NZ - NEAR):
        pl.semaphore_signal(
            known, inc=1, device_id=at_z(lax.rem(z + step, NZ)), device_id_type=MESH
        )
    loop(1, 8, lambda i: disp_copy(i, lax.rem(e + 8 - i, 8)).wait())

    xt = jnp.transpose(disp[:, 0:TB, :].reshape(NT, 128))
    gt = jnp.transpose(disp[:, TB : 2 * TB, :].reshape(NT, 128))
    row = lax.broadcasted_iota(jnp.int32, (32, NT), 0)
    tail = xt[FD:128, :].astype(F32)
    weight = jnp.sum(jnp.where((row == e) | (row == e + 8), tail, 0.0), axis=0, keepdims=True)
    xj[...] = xt[0:FD, :]
    gj[...] = gt[0:FD, :]
    for half in range(2):
        for th in range(2):
            cut = slice(128 * th, 128 * th + 128)
            rows = slice(HR * half, HR * half + HR)
            own[th, half] = xt[rows, cut]
            own[2 + th, half] = gt[rows, cut]
    gat[x, y, z, c] = own[x, c]

    pl.semaphore_wait(known, 2)

    def z_copy(of, to):
        piece = gat.at[x, y, of, c]
        return remote(piece, piece, z_ss.at[to], z_rs.at[of], at_z(to))

    group = z // 4
    for off in (0, 3, 1, 2):

        def z_start(i):
            to = 4 * lax.rem(group + off, 4) + i

            @pl.when(to != z)
            def _():
                z_copy(z, to).start()

        loop(0, 4, z_start)

    def sum_start(n, value):
        for k in range(NZ):
            part[n, k] = value[8 * (k // 2) : 8 * (k // 2) + 8, 128 * (k % 2) : 128 * (k % 2) + 128]
        rsb[n, z] = part[n, z]

        def go(i):
            to = lax.rem(z + i, NZ)
            remote(part.at[n, to], rsb.at[n, z], r_ss.at[n, i], r_rs.at[n, i], at_z(to)).start()

        loop(1, NZ, go)

    def y_copy(n, i, slot):
        return remote(
            ysend.at[n], yrec.at[n, slot], y_ss.at[n, i], y_rs.at[n, i], at_y(lax.rem(y + i, NY))
        )

    def sum_middle(n):
        def done(i):
            to = lax.rem(z + i, NZ)
            remote(
                part.at[n, to],
                rsb.at[n, lax.rem(z + NZ - i, NZ)],
                r_ss.at[n, i],
                r_rs.at[n, i],
                at_z(to),
            ).wait()

        loop(1, NZ, done)
        total = jnp.sum(rsb[n], axis=0)
        ysend[n] = total
        yrec[n, y] = total
        loop(1, NY, lambda i: y_copy(n, i, y).start())

    def g_copy(n, i, slot):
        piece = full.at[n, slot]
        return remote(piece, piece, g_ss.at[n, i], g_rs.at[n, i], at_z(lax.rem(z + i, NZ)))

    def sum_last(n):
        loop(1, NY, lambda i: y_copy(n, i, lax.rem(y + NY - i, NY)).wait())
        full[n, z] = jnp.sum(yrec[n], axis=0)
        loop(1, NZ, lambda i: g_copy(n, i, z).start())

    def sum_done(n):
        loop(1, NZ, lambda i: g_copy(n, i, lax.rem(z + NZ - i, NZ)).wait())
        return jnp.concatenate(
            [jnp.concatenate([full[n, 2 * k], full[n, 2 * k + 1]], axis=1) for k in range(8)], axis=0
        )

    a13t = jnp.concatenate([a1t[0], a3t[0]], axis=0)
    sum_start(
        0,
        jnp.concatenate(
            [dot_nn(a13t, xj[...]), dot_nn(rj[0], gj[...]), jnp.zeros((16, NT), F32)], axis=0
        ),
    )

    ahead_x = lax.rem(x + 1 + 2 * c, NX)
    behind_x = lax.rem(x + 3 + 2 * c, NX)
    far_x = lax.rem(x + 2, NX)
    ahead_y = lax.rem(y + 1 + 2 * c, NY)
    behind_y = lax.rem(y + 3 + 2 * c, NY)
    far_y = lax.rem(y + 2, NY)

    def group_of(s):
        n = s // 2
        return lax.rem(group + n + n // 2 - 2 * (n // 3), 4)

    def z_of(s, k):
        return 4 * group_of(s) + 2 * lax.rem(s, 2) + k

    def a1_copy(k, s, of, to):
        piece = gat.at[of, y, z_of(s, 0), c]
        return remote(piece, piece, a1_ss.at[k, s], a1_rs.at[k, s], at_x(to))

    def b1_copy(k, s, of, to):
        piece = gat.at[x, of, z_of(s, 1), c]
        return remote(piece, piece, b1_ss.at[k, s], b1_rs.at[k, s], at_y(to))

    def a2_copy(k, s, of, to):
        piece = gat.at[:, of, z_of(s, 0), c]
        return remote(piece, piece, a2_ss.at[k, s], a2_rs.at[k, s], at_y(to))

    def b2_copy(k, s, of, to):
        piece = gat.at[of, :, z_of(s, 1), c]
        return remote(piece, piece, b2_ss.at[k, s], b2_rs.at[k, s], at_x(to))

    def sa_copy(k, s, of, core):
        piece = gat.at[:, of, z_of(s, 0), core]
        return remote(piece, piece, s1_ss.at[k, s], s1_rs.at[k, s], sib)

    def sb_copy(k, s, of, core):
        piece = gat.at[of, :, z_of(s, 1), core]
        return remote(piece, piece, s2_ss.at[k, s], s2_rs.at[k, s], sib)

    def narrow_start(s):
        for k in range(2):
            of = z_of(s, k)

            @pl.when(of != z)
            def _():
                z_copy(of, z).wait_recv()

        a1_copy(0, s, x, ahead_x).start()
        b1_copy(0, s, y, ahead_y).start()
        a1_copy(1, s, x, behind_x).start()
        b1_copy(1, s, y, behind_y).start()

    def narrow_pass(s):
        a1_copy(0, s, behind_x, ahead_x).wait_recv()
        a1_copy(2, s, behind_x, ahead_x).start()
        b1_copy(0, s, behind_y, ahead_y).wait_recv()
        b1_copy(2, s, behind_y, ahead_y).start()

    def wide_start(s):
        a1_copy(1, s, ahead_x, behind_x).wait_recv()
        a1_copy(2, s, far_x, ahead_x).wait_recv()
        a2_copy(0, s, y, ahead_y).start()
        a2_copy(1, s, y, behind_y).start()
        b1_copy(1, s, ahead_y, behind_y).wait_recv()
        b1_copy(2, s, far_y, ahead_y).wait_recv()
        b2_copy(0, s, x, ahead_x).start()
        b2_copy(1, s, x, behind_x).start()
        sa_copy(0, s, y, c).start()
        sb_copy(0, s, x, c).start()

    def wide_pass(s):
        a2_copy(0, s, behind_y, ahead_y).wait_recv()
        a2_copy(2, s, behind_y, ahead_y).start()
        b2_copy(0, s, behind_x, ahead_x).wait_recv()
        b2_copy(2, s, behind_x, ahead_x).start()
        sa_copy(1, s, behind_y, c).start()
        sb_copy(1, s, behind_x, c).start()
        a2_copy(1, s, ahead_y, behind_y).wait_recv()
        sa_copy(2, s, ahead_y, c).start()
        b2_copy(1, s, ahead_x, behind_x).wait_recv()
        sb_copy(2, s, ahead_x, c).start()

    def wide_end(s):
        a2_copy(2, s, far_y, ahead_y).wait_recv()
        sa_copy(3, s, far_y, c).start()
        b2_copy(2, s, far_x, ahead_x).wait_recv()
        sb_copy(3, s, far_x, c).start()

    def core_end(s):
        for k, (fy, fx) in enumerate(
            ((y, x), (ahead_y, ahead_x), (behind_y, behind_x), (far_y, far_x))
        ):
            sa_copy(k, s, fy, 1 - c).wait()
            sb_copy(k, s, fx, 1 - c).wait()

    def project(s):
        g = group_of(s)

        def one(yy):
            cols = pl.ds(pl.multiple_of((4 * yy + g) * STEP, 128), STEP)

            def side(n):
                return gat[n, yy, pl.ds(4 * g, 4)].reshape(STEP, 128)

            acch[...] += dot_nn(w13t[:, cols], jnp.concatenate([side(0), side(1)], axis=1))
            accq[...] += dot_nn(w2[:, cols], jnp.concatenate([side(2), side(3)], axis=1))

        loop(0, NY, one)

    acch[...] = jnp.zeros_like(acch)
    accq[...] = jnp.zeros_like(accq)

    def at_tick(t, lag, body):
        @pl.when((t >= lag) & (t < lag + 8))
        def _():
            body(t - lag)

    def gather_tick(t):
        at_tick(t, 0, narrow_start)
        at_tick(t, 2, narrow_pass)
        at_tick(t, 4, wide_start)
        at_tick(t, 6, wide_pass)
        at_tick(t, 8, wide_end)
        at_tick(t, 9, core_end)
        at_tick(t, 0, lambda s: loop(6 * s, 6 * s + 6, flip))

        @pl.when((t >= 9) & (lax.rem(t, 2) == 0))
        def _():
            project(t - 9)

        @pl.when(t == 6)
        def _():
            sum_middle(0)

        @pl.when(t == 9)
        def _():
            sum_last(0)

    loop(0, 17, gather_tick)

    low_sums = sum_done(0)
    u1 = low_sums[0:16].astype(BF16)
    u3 = low_sums[16:32].astype(BF16)
    v = low_sums[32:48]
    h1 = acch[0:HID] + SCALE * dot_tn(b1[0], u1)
    h3 = acch[HID : 2 * HID] + SCALE * dot_tn(b3[0], u3)
    q = accq[...] + SCALE * dot_tn(d1t[0], v.astype(BF16))
    sig = jax.nn.sigmoid(h1)
    active = h1 * sig
    slope = sig * (1.0 + h1 * (1.0 - sig))
    hidden = (active * h3).astype(BF16)
    back = weight * q
    e1 = (back * h3 * slope).astype(BF16)
    e3 = (back * active).astype(BF16)
    kk = jnp.sum(hidden.astype(F32) * q, axis=0, keepdims=True)
    et[0:HID, :] = e1
    et[HID : 2 * HID, :] = e3
    sum_start(
        1,
        jnp.concatenate(
            [
                dot_nn(b1[0], e1),
                dot_nn(b3[0], e3),
                dot_nn(d1t[0], hidden),
                kk,
                jnp.zeros((15, NT), F32),
            ],
            axis=0,
        ),
    )

    def group_at(s):
        return lax.rem(group + 2 + s + (s // 2) * (1 - 2 * s), 4)

    def piece_z(s, k, core):
        return 4 * group_at(s) + 2 * core + k

    def k_copy(s, core):
        return remote(
            yb.at[:, :, pl.ds(piece_z(s, 0, core), 2)], rc.at[s], k_ss.at[s], k_rs.at[s], sib
        )

    def grads(s):
        g = group_at(s)

        def one(yy):
            rows = pl.ds(pl.multiple_of((4 * yy + g) * STEP, STEP), STEP)
            pair = jnp.concatenate([w1[rows, :], w3[rows, :]], axis=1)
            out = dot_nn(pair, et[...]).astype(BF16).reshape(4, 2, HR, NT)
            for rh in range(2):
                for th in range(2):
                    yb[2 * rh + th, yy, pl.ds(4 * g, 4)] = out[:, rh, :, 128 * th : 128 * th + 128]

        loop(0, NY, one)
        k_copy(s, 1 - c).start()

    def xo_copy(s):
        return remote(
            yb.at[far_x, :, piece_z(s, 0, c)], axo.at[s], p1_ss.at[0, s], p1_rs.at[0, s], at_x(ahead_x)
        )

    def yo_copy(s):
        return remote(
            yb.at[:, far_y, piece_z(s, 1, c)], byo.at[s], p1_ss.at[1, s], p1_rs.at[1, s], at_y(ahead_y)
        )

    def xr_copy(k, s, to):
        return remote(
            yb.at[to, :, piece_z(s, 0, c)], axr.at[k, s], p1_ss.at[2 + k, s], p1_rs.at[2 + k, s], at_x(to)
        )

    def yr_copy(k, s, to):
        return remote(
            yb.at[:, to, piece_z(s, 1, c)], byr.at[k, s], p1_ss.at[4 + k, s], p1_rs.at[4 + k, s], at_y(to)
        )

    def add_core(s):
        k_copy(s, 1 - c).wait()

        def one(xx):
            zs = pl.ds(piece_z(s, 0, c), 2)
            both = yb[xx, :, zs].astype(F32) + rc[s, xx].astype(F32)
            yb[xx, :, zs] = both.astype(BF16)

        loop(0, NX, one)
        xo_copy(s).start()
        yo_copy(s).start()
        xr_copy(1, s, behind_x).start()
        yr_copy(1, s, behind_y).start()

    def add_far(s):
        za = piece_z(s, 0, c)
        zb = piece_z(s, 1, c)
        xo_copy(s).wait_recv()
        yb[ahead_x, :, za] = (yb[ahead_x, :, za].astype(F32) + axo[s].astype(F32)).astype(BF16)
        xr_copy(0, s, ahead_x).start()
        yo_copy(s).wait_recv()
        yb[:, ahead_y, zb] = (yb[:, ahead_y, zb].astype(F32) + byo[s].astype(F32)).astype(BF16)
        yr_copy(0, s, ahead_y).start()

    def qy_copy(s, i):
        to = lax.rem(y + i, NY)
        return remote(ya.at[s, to], ayb.at[s, i], p2_ss.at[0, s, i], p2_rs.at[0, s, i], at_y(to))

    def qx_copy(s, i):
        to = lax.rem(x + i, NX)
        return remote(yc.at[s, to], bxb.at[s, i], p2_ss.at[1, s, i], p2_rs.at[1, s, i], at_x(to))

    def add_first(s):
        xr_copy(0, s, ahead_x).wait_recv()
        xr_copy(1, s, behind_x).wait_recv()
        ya[s] = (
            yb[x, :, piece_z(s, 0, c)].astype(F32) + axr[0, s].astype(F32) + axr[1, s].astype(F32)
        ).astype(BF16)
        for i in (2, 1, 3):
            qy_copy(s, i).start()
        yr_copy(0, s, ahead_y).wait_recv()
        yr_copy(1, s, behind_y).wait_recv()
        yc[s] = (
            yb[:, y, piece_z(s, 1, c)].astype(F32) + byr[0, s].astype(F32) + byr[1, s].astype(F32)
        ).astype(BF16)
        for i in (2, 1, 3):
            qx_copy(s, i).start()

    def t_copy(s, k):
        to = piece_z(s, k, c)
        return remote(zsend.at[s, k], zr.at[z], p3_ss.at[2 * s + k], p3_rs.at[z], at_z(to))

    def add_second(s):
        for k in range(2):
            for i in (1, 3, 2):
                if k == 0:
                    qy_copy(s, i).wait()
                else:
                    qx_copy(s, i).wait()
            piece = (ya[s, y] if k == 0 else yc[s, x]).astype(F32)
            for i in (1, 2, 3):
                piece = piece + (ayb[s, i] if k == 0 else bxb[s, i]).astype(F32)
            zsend[s, k] = piece.astype(BF16)
            to = piece_z(s, k, c)

            @pl.when(to != z)
            def _():
                t_copy(s, k).start()

            @pl.when(to == z)
            def _():
                zr[z] = zsend[s, k]

    def at_step(t, lag, body):
        @pl.when((t >= lag) & (t < lag + 4))
        def _():
            body(t - lag)

    def scatter_tick(t):
        at_step(t, 0, grads)
        at_step(t, 4, add_second)
        at_step(t, 3, add_first)
        at_step(t, 2, add_far)
        at_step(t, 1, add_core)

        @pl.when(t == 3)
        def _():
            sum_middle(1)

        @pl.when(t == 4)
        def _():
            dft[0] = SCALE * dot_nt((weight * v).astype(BF16), hidden)
            gs[0] = SCALE * dot_nt(u1, e1)
            us[0] = SCALE * dot_nt(u3, e3)

        @pl.when(t == 5)
        def _():
            sum_last(1)

    loop(0, 8, scatter_tick)

    holder = lax.rem(z, 4) // 2 == c
    sums = sum_done(1)
    r13 = sums[0:32].astype(BF16)
    zt = (weight * sums[32:48]).astype(BF16)
    ascr[FD:128, :] = jnp.zeros((128 - FD, NT), F32)
    ascr[0:FD, :] = SCALE * dot_tn(a13t, r13)
    ascr[FD : FD + 1, :] = sums[48:49]
    asend[...] = jnp.transpose(ascr[...]).astype(BF16).reshape(8, TB, 128)
    afin[e] = asend[e]

    def h_copy(i, slot):
        to = lax.rem(e + i, 8)
        return remote(asend.at[to], afin.at[slot], h_ss.at[i], h_rs.at[i], (to, j))

    loop(1, 8, lambda i: h_copy(i, e).start())
    first = SCALE * dot_nt(r13, xj[...])
    gft[0] = first[0:16]
    uft[0] = first[16:32]
    ds[0] = SCALE * dot_nt(zt, gj[...])

    rh = x // 2
    th = lax.rem(x, 2)

    def f_copy(i):
        return remote(fsend.at[i], fin.at[rh], f_ss.at[i], f_rs.at[rh], (4 * th + i, j))

    @pl.when(holder)
    def _():
        def got(i):
            of = lax.rem(z + i, NZ)
            remote(zsend.at[0, 0], zr.at[of], p3_ss.at[0], p3_rs.at[of], at_z(of)).wait_recv()

        loop(1, NZ, got)
        fscr[...] = jnp.zeros_like(fscr)
        fscr[pl.ds(pl.multiple_of(HR * rh, HR), HR), :] = jnp.sum(zr[...].astype(F32), axis=0)
        fsend[...] = jnp.transpose(fscr[...]).astype(BF16).reshape(4, TB, 128)
        for i in range(4):

            @pl.when(4 * th + i == e)
            def _():
                fin[rh] = fsend[i]

            @pl.when(4 * th + i != e)
            def _():
                f_copy(i).start()

    loop(1, 8, lambda i: h_copy(i, lax.rem(e + 8 - i, 8)).wait())

    total = jnp.zeros((TB, 128), F32)
    first_k = jnp.zeros((TB, 1), F32)
    second_k = jnp.zeros((TB, 1), F32)
    for n in range(8):
        block = afin[n].astype(F32)
        total = total + block
        column = block[:, FD : FD + 1]
        first_k = first_k + jnp.where(id0 == n, column, 0.0)
        second_k = second_k + jnp.where(id1 == n, column, 0.0)
    lane = lax.broadcasted_iota(jnp.int32, (TB, 128), 1)
    both_k = jnp.where(lane == 0, first_k, 0.0) + jnp.where(lane == 1, second_k, 0.0)
    cg[...] = jnp.transpose(both_k)[0:2, :]

    for n in range(2):

        @pl.when(4 * n + 2 * (e // 4) + lax.rem(z, 4) // 2 != e)
        def _():
            remote(fsend.at[0], fin.at[n], f_ss.at[0], f_rs.at[n], (e, j)).wait_recv()

    total = total + fin[0].astype(F32) + fin[1].astype(F32)
    tg[...] = total[:, 0:FD].astype(BF16)

    @pl.when(holder)
    def _():
        for i in range(4):

            @pl.when(4 * th + i != e)
            def _():
                f_copy(i).wait_send()

    def z_sent(i):
        z_copy(z, lax.rem(z + i, NZ)).wait_send()

    loop(1, NZ, z_sent)

    def gather_sent(s):
        for k in range(3):
            a1_copy(k, s, x, ahead_x).wait_send()
            b1_copy(k, s, y, ahead_y).wait_send()
            a2_copy(k, s, y, ahead_y).wait_send()
            b2_copy(k, s, x, ahead_x).wait_send()

    loop(0, 8, gather_sent)

    def scatter_sent(s):
        xo_copy(s).wait_send()
        yo_copy(s).wait_send()
        for k in range(2):
            xr_copy(k, s, ahead_x).wait_send()
            yr_copy(k, s, ahead_y).wait_send()

            @pl.when(piece_z(s, k, c) != z)
            def _():
                t_copy(s, k).wait_send()

    loop(0, 4, scatter_sent)


def finish(*refs):
    sems = refs[16]
    copies = [pltpu.make_async_copy(refs[n], refs[8 + n], sems.at[n]) for n in range(8)]
    for copy in copies:
        copy.start()
    for copy in copies:
        copy.wait()


def local(
    tokens,
    upstream,
    expert_ids,
    slot_pos,
    combine,
    gate_weight,
    upward_weight,
    down_weight,
    gate_adapter_first,
    gate_adapter_second,
    upward_adapter_first,
    upward_adapter_second,
    down_adapter_first,
    down_right,
):
    vmem = pl.BlockSpec(memory_space=pltpu.VMEM)
    hbm = pl.BlockSpec(memory_space=pl.ANY)
    dma = pltpu.SemaphoreType.DMA

    def buf(shape, dtype=BF16):
        return pltpu.VMEM(shape, dtype)

    outs = pl.pallas_call(
        kernel,
        out_shape=(
            jax.ShapeDtypeStruct((TB, FD), BF16),
            jax.ShapeDtypeStruct((2, TB), F32),
            jax.ShapeDtypeStruct((1, 16, FD), F32),
            jax.ShapeDtypeStruct((1, 16, HID), F32),
            jax.ShapeDtypeStruct((1, 16, FD), F32),
            jax.ShapeDtypeStruct((1, 16, HID), F32),
            jax.ShapeDtypeStruct((1, 16, HID), F32),
            jax.ShapeDtypeStruct((1, 16, FD), F32),
        ),
        in_specs=[hbm] * 13,
        out_specs=[vmem] * 8,
        scratch_shapes=[
            buf((TB, FD)),
            buf((TB, FD)),
            buf((2, TB), jnp.int32),
            buf((2, TB), F32),
            buf((1, 16, FD)),
            buf((1, 16, HID)),
            buf((1, 16, FD)),
            buf((1, 16, HID)),
            buf((1, 16, HID)),
            buf((1, 16, FD)),
            buf((6144, HID)),
            buf((6144, HID)),
            buf((HID, 6144)),
            buf((2 * HID, 6144)),
            buf((128, 128), F32),
            buf((2 * TB, 128)),
            buf((8, 2 * TB, 128)),
            buf((FD, NT)),
            buf((FD, NT)),
            buf((NX, NC, HR, 128)),
            buf((NX, NY, NZ, NC, HR, 128)),
            buf((2 * HID, NT), F32),
            buf((HID, NT), F32),
            buf((2 * HID, NT)),
            buf((2, NZ, 8, 128), F32),
            buf((2, NZ, 8, 128), F32),
            buf((2, 8, 128), F32),
            buf((2, NY, 8, 128), F32),
            buf((2, NZ, 8, 128), F32),
            buf((NX, NY, NZ, HR, 128)),
            buf((4, NX, NY, 2, HR, 128)),
            buf((4, NY, HR, 128)),
            buf((4, NX, HR, 128)),
            buf((2, 4, NY, HR, 128)),
            buf((2, 4, NX, HR, 128)),
            buf((4, NY, HR, 128)),
            buf((4, NX, HR, 128)),
            buf((4, 4, HR, 128)),
            buf((4, 4, HR, 128)),
            buf((4, 2, HR, 128)),
            buf((NZ, HR, 128)),
            buf((128, 128), F32),
            buf((4, TB, 128)),
            buf((2, TB, 128)),
            buf((128, NT), F32),
            buf((8, TB, 128)),
            buf((8, TB, 128)),
            dma((13,)),
            dma((8,)),
            dma((8,)),
            dma((NZ,)),
            dma((NZ,)),
            dma((3, 8)),
            dma((3, 8)),
            dma((3, 8)),
            dma((3, 8)),
            dma((3, 8)),
            dma((3, 8)),
            dma((3, 8)),
            dma((3, 8)),
            dma((4, 8)),
            dma((4, 8)),
            dma((4, 8)),
            dma((4, 8)),
            dma((2, NZ)),
            dma((2, NZ)),
            dma((2, NY)),
            dma((2, NY)),
            dma((2, NZ)),
            dma((2, NZ)),
            dma((4,)),
            dma((4,)),
            dma((6, 4)),
            dma((6, 4)),
            dma((2, 4, 4)),
            dma((2, 4, 4)),
            dma((8,)),
            dma((NZ,)),
            dma((4,)),
            dma((2,)),
            dma((8,)),
            dma((8,)),
            pltpu.SemaphoreType.REGULAR,
        ],
        compiler_params=pltpu.CompilerParams(
            collective_id=0, has_side_effects=True, vmem_limit_bytes=GRANT
        ),
        name="moe_backward",
    )(
        tokens,
        upstream,
        jnp.transpose(expert_ids),
        jnp.transpose(combine),
        gate_weight,
        upward_weight,
        down_weight,
        jnp.swapaxes(gate_adapter_first, 1, 2),
        gate_adapter_second,
        jnp.swapaxes(upward_adapter_first, 1, 2),
        upward_adapter_second,
        jnp.swapaxes(down_adapter_first, 1, 2),
        down_right,
    )
    token_grads, combine_grads, gft, gs, uft, us, dft, ds = pl.pallas_call(
        finish,
        out_shape=[jax.ShapeDtypeStruct(o.shape, o.dtype) for o in outs],
        in_specs=[hbm] * 8,
        out_specs=[hbm] * 8,
        scratch_shapes=[dma((8,))],
        compiler_params=pltpu.CompilerParams(vmem_limit_bytes=GRANT),
        name="hand_over",
    )(*outs)
    return (
        token_grads,
        jnp.transpose(combine_grads),
        jnp.swapaxes(gft, 1, 2),
        gs,
        jnp.swapaxes(uft, 1, 2),
        us,
        jnp.swapaxes(dft, 1, 2),
        ds,
    )


def solution(mesh):
    in_specs = (
        P("expert", "tensor"),
        P("expert", "tensor"),
        P("expert", None),
        P("expert", None),
        P("expert", None),
        P("expert", None, "tensor"),
        P("expert", None, "tensor"),
        P("expert", "tensor", None),
        P("expert", "tensor", None),
        P("expert", None, "tensor"),
        P("expert", "tensor", None),
        P("expert", None, "tensor"),
        P("expert", "tensor", None),
        P("expert", None, "tensor"),
    )
    out_specs = (
        P("expert", "tensor"),
        P("expert", None),
        P("expert", "tensor", None),
        P("expert", None, "tensor"),
        P("expert", "tensor", None),
        P("expert", None, "tensor"),
        P("expert", "tensor", None),
        P("expert", None, "tensor"),
    )
    return jax.shard_map(local, mesh=mesh, in_specs=in_specs, out_specs=out_specs, check_vma=False)
```

```python
import jax
import jax.numpy as jnp
from jax import lax
from jax.experimental import pallas as pl
from jax.experimental.pallas import tpu as pltpu
from jax.sharding import PartitionSpec as P

MESH = pl.DeviceIdType.MESH
F32 = jnp.float32
BF16 = jnp.bfloat16
SCALE = 2.0
NX, NY, NZ, NC = 4, 4, 16, 2
TB = 32
FD = 96
HR = 48
HID = 128
NT = 256
STEP = 4 * FD
GRANT = 60 * 2**20
NEAR = 4


def dot_nn(a, b):
    return lax.dot_general(a, b, (((1,), (0,)), ((), ())), preferred_element_type=F32)


def dot_nt(a, b):
    return lax.dot_general(a, b, (((1,), (1,)), ((), ())), preferred_element_type=F32)


def dot_tn(a, b):
    return lax.dot_general(a, b, (((0,), (0,)), ((), ())), preferred_element_type=F32)


def remote(src, dst, send, recv, dev):
    return pltpu.make_async_remote_copy(
        src_ref=src, dst_ref=dst, send_sem=send, recv_sem=recv, device_id=dev, device_id_type=MESH
    )


def loop(low, high, body):
    def step(i, carry):
        body(i)
        return carry

    lax.fori_loop(low, high, step, 0)


def kernel(
    tok_hbm,
    ups_hbm,
    ids_hbm,
    comb_hbm,
    w1_hbm,
    w3_hbm,
    w2_hbm,
    a1t_hbm,
    b1_hbm,
    a3t_hbm,
    b3_hbm,
    d1t_hbm,
    rj_hbm,
    tg,
    cg,
    gft,
    gs,
    uft,
    us,
    dft,
    ds,
    tok,
    ups,
    ids,
    comb,
    a1t,
    b1,
    a3t,
    b3,
    d1t,
    rj,
    w1,
    w3,
    w2,
    w13t,
    wide_t,
    src,
    disp,
    xj,
    gj,
    own,
    gat,
    acch,
    accq,
    et,
    part,
    rsb,
    ysend,
    yrec,
    full,
    yb,
    rc,
    axo,
    byo,
    axr,
    byr,
    ya,
    yc,
    ayb,
    bxb,
    zsend,
    zr,
    fscr,
    fsend,
    fin,
    ascr,
    asend,
    afin,
    w_sem,
    d_ss,
    d_rs,
    z_ss,
    z_rs,
    n_ss,
    n_rs,
    w_ss,
    w_rs,
    c_ss,
    c_rs,
    r_ss,
    r_rs,
    y_ss,
    y_rs,
    g_ss,
    g_rs,
    k_ss,
    k_rs,
    p1_ss,
    p1_rs,
    p2_ss,
    p2_rs,
    p3_ss,
    p3_rs,
    f_ss,
    f_rs,
    h_ss,
    h_rs,
    known,
):
    e = lax.axis_index("expert")
    j = lax.axis_index("tensor")
    x = e // 2
    c = lax.rem(e, 2)
    y = j // NZ
    z = lax.rem(j, NZ)
    sib = (2 * x + 1 - c, j)

    def at_x(v):
        return (2 * v + c, j)

    def at_y(v):
        return (e, v * NZ + z)

    def at_z(v):
        return (e, y * NZ + v)

    def arrived(ref, sem):
        remote(ref, ref, sem, sem, sib).wait_recv()

    def left(ref, sem):
        remote(ref, ref, sem, sem, sib).wait_send()

    def pieces(n):
        return gat.at[0, 0, 0:n, 0]

    bar = pltpu.get_barrier_semaphore()

    def sig_e(i):
        pl.semaphore_signal(bar, inc=1, device_id=(lax.rem(e + i, 8), j), device_id_type=MESH)

    def sig_z(i):
        pl.semaphore_signal(bar, inc=1, device_id=at_z(lax.rem(z + i, NZ)), device_id_type=MESH)

    def sig_y(i):
        pl.semaphore_signal(bar, inc=1, device_id=at_y(lax.rem(y + i, NY)), device_id_type=MESH)

    loop(1, NEAR + 1, sig_z)
    loop(NZ - NEAR, NZ, sig_z)
    loop(1, NY, sig_y)
    loop(1, 8, sig_e)

    pairs = [
        (tok_hbm, tok),
        (ups_hbm, ups),
        (ids_hbm, ids),
        (comb_hbm, comb),
        (a1t_hbm, a1t),
        (b1_hbm, b1),
        (a3t_hbm, a3t),
        (b3_hbm, b3),
        (d1t_hbm, d1t),
        (rj_hbm, rj),
        (w1_hbm.at[0], w1),
        (w3_hbm.at[0], w3),
        (w2_hbm.at[0], w2),
    ]
    loads = [pltpu.make_async_copy(a, b, w_sem.at[n]) for n, (a, b) in enumerate(pairs)]
    for load in loads:
        load.start()
    for load in loads[0:4]:
        load.wait()

    expert_row = lax.broadcasted_iota(jnp.int32, (8, TB), 0)
    dense = jnp.zeros((8, TB), F32)
    for k in range(2):
        dense = dense + jnp.where(expert_row == ids[k : k + 1, :], comb[k : k + 1, :], 0.0)
    high = dense.astype(BF16).astype(F32)
    wide_t[...] = jnp.zeros_like(wide_t)
    wide_t[0:2, 0:TB] = ids[...].astype(F32)
    wide_t[FD : FD + 8, 0:TB] = high
    wide_t[FD + 8 : FD + 16, 0:TB] = dense - high
    wide = jnp.transpose(wide_t[...])[0:TB, :]
    id0 = wide[:, 0:1]
    id1 = wide[:, 1:2]
    src[0:TB, :] = wide.astype(BF16)
    src[0:TB, 0:FD] = tok[...]
    src[TB : 2 * TB, :] = jnp.zeros((TB, 128), BF16)
    src[TB : 2 * TB, 0:FD] = ups[...]
    disp[e] = src[...]
    for load in loads[4:]:
        load.wait()

    def flip(i):
        rows = pl.ds(pl.multiple_of(i * 128, 128), 128)
        w13t[0:HID, rows] = jnp.transpose(w1[rows, :])
        w13t[HID : 2 * HID, rows] = jnp.transpose(w3[rows, :])


    loop(0, 24, flip)
    pl.semaphore_wait(bar, 7 + 2 * NEAR + NY - 1)

    def disp_copy(i, slot):
        return remote(
            src, disp.at[slot], d_ss.at[0], d_rs.at[0], (lax.rem(e + i, 8), j)
        )

    loop(1, 8, lambda i: disp_copy(i, e).start())
    for step in (NEAR, NZ - NEAR):
        pl.semaphore_signal(
            known, inc=1, device_id=at_z(lax.rem(z + step, NZ)), device_id_type=MESH
        )
    arrived(disp.at[0:7], d_rs.at[0])

    xt = jnp.transpose(disp[:, 0:TB, :].reshape(NT, 128))
    gt = jnp.transpose(disp[:, TB : 2 * TB, :].reshape(NT, 128))
    row = lax.broadcasted_iota(jnp.int32, (32, NT), 0)
    tail = xt[FD:128, :].astype(F32)
    weight = jnp.sum(jnp.where((row == e) | (row == e + 8), tail, 0.0), axis=0, keepdims=True)
    xj[...] = xt[0:FD, :]
    gj[...] = gt[0:FD, :]
    for half in range(2):
        for th in range(2):
            cut = slice(128 * th, 128 * th + 128)
            rows = slice(HR * half, HR * half + HR)
            own[th, half] = xt[rows, cut]
            own[2 + th, half] = gt[rows, cut]
    gat[x, y, z, c] = own[x, c]

    pl.semaphore_wait(known, 2)

    def z_copy(of, to):
        piece = gat.at[x, y, of, c]
        return remote(piece, piece, z_ss.at[0], z_rs.at[of], at_z(to))

    group = z // 4
    for off in (0, 3, 1, 2):

        def z_start(i):
            to = 4 * lax.rem(group + off, 4) + i

            @pl.when(to != z)
            def _():
                z_copy(z, to).start()

        loop(0, 4, z_start)

    def sum_start(n, value):
        for k in range(NZ):
            part[n, k] = value[8 * (k // 2) : 8 * (k // 2) + 8, 128 * (k % 2) : 128 * (k % 2) + 128]
        rsb[n, z] = part[n, z]

        def go(i):
            to = lax.rem(z + i, NZ)
            remote(part.at[n, to], rsb.at[n, z], r_ss.at[n], r_rs.at[n], at_z(to)).start()

        loop(1, NZ, go)

    def y_copy(n, i, slot):
        return remote(
            ysend.at[n], yrec.at[n, slot], y_ss.at[n], y_rs.at[n], at_y(lax.rem(y + i, NY))
        )

    def sum_middle(n):
        arrived(rsb.at[n, 0 : NZ - 1], r_rs.at[n])
        total = jnp.sum(rsb[n], axis=0)
        ysend[n] = total
        yrec[n, y] = total
        loop(1, NY, lambda i: y_copy(n, i, y).start())

    def g_copy(n, i, slot):
        piece = full.at[n, slot]
        return remote(piece, piece, g_ss.at[n], g_rs.at[n], at_z(lax.rem(z + i, NZ)))

    def sum_last(n):
        arrived(yrec.at[n, 0 : NY - 1], y_rs.at[n])
        full[n, z] = jnp.sum(yrec[n], axis=0)
        loop(1, NZ, lambda i: g_copy(n, i, z).start())

    def sum_done(n):
        arrived(full.at[n, 0 : NZ - 1], g_rs.at[n])
        return jnp.concatenate(
            [jnp.concatenate([full[n, 2 * k], full[n, 2 * k + 1]], axis=1) for k in range(8)], axis=0
        )

    a13t = jnp.concatenate([a1t[0], a3t[0]], axis=0)
    sum_start(
        0,
        jnp.concatenate(
            [dot_nn(a13t, xj[...]), dot_nn(rj[0], gj[...]), jnp.zeros((16, NT), F32)], axis=0
        ),
    )

    ahead_x = lax.rem(x + 1 + 2 * c, NX)
    behind_x = lax.rem(x + 3 + 2 * c, NX)
    far_x = lax.rem(x + 2, NX)
    ahead_y = lax.rem(y + 1 + 2 * c, NY)
    behind_y = lax.rem(y + 3 + 2 * c, NY)
    far_y = lax.rem(y + 2, NY)

    def group_of(s):
        n = s // 2
        return lax.rem(group + n + n // 2 - 2 * (n // 3), 4)

    def z_of(s, k):
        return 4 * group_of(s) + 2 * lax.rem(s, 2) + k

    def a1_copy(k, s, of, to):
        piece = gat.at[of, y, z_of(s, 0), c]
        return remote(piece, piece, n_ss.at[0], n_rs.at[(k + 1) // 2, s], at_x(to))

    def b1_copy(k, s, of, to):
        piece = gat.at[x, of, z_of(s, 1), c]
        return remote(piece, piece, n_ss.at[0], n_rs.at[(k + 1) // 2, s], at_y(to))

    def a2_copy(k, s, of, to):
        piece = gat.at[:, of, z_of(s, 0), c]
        return remote(piece, piece, w_ss.at[0], w_rs.at[(k + 1) // 2, s], at_y(to))

    def b2_copy(k, s, of, to):
        piece = gat.at[of, :, z_of(s, 1), c]
        return remote(piece, piece, w_ss.at[0], w_rs.at[(k + 1) // 2, s], at_x(to))

    def core_copy(s):
        piece = gat.at[:, :, pl.ds(z_of(s, 0), 2), c]
        return remote(piece, piece, c_ss.at[0], c_rs.at[s], sib)

    def narrow_start(s):
        for k in range(2):
            of = z_of(s, k)

            @pl.when(of != z)
            def _():
                z_copy(of, z).wait_recv()

        a1_copy(0, s, x, ahead_x).start()
        b1_copy(0, s, y, ahead_y).start()
        a1_copy(1, s, x, behind_x).start()
        b1_copy(1, s, y, behind_y).start()

    def narrow_pass(s):
        arrived(pieces(2), n_rs.at[0, s])
        a1_copy(2, s, behind_x, ahead_x).start()
        b1_copy(2, s, behind_y, ahead_y).start()

    def wide_start(s):
        arrived(pieces(4), n_rs.at[1, s])
        a2_copy(0, s, y, ahead_y).start()
        b2_copy(0, s, x, ahead_x).start()
        a2_copy(1, s, y, behind_y).start()
        b2_copy(1, s, x, behind_x).start()

    def wide_pass(s):
        arrived(pieces(8), w_rs.at[0, s])
        a2_copy(2, s, behind_y, ahead_y).start()
        b2_copy(2, s, behind_x, ahead_x).start()

    def wide_end(s):
        arrived(pieces(16), w_rs.at[1, s])
        core_copy(s).start()

    def core_end(s):
        core_copy(s).wait_recv()

    def project(s):
        g = group_of(s)

        def one(yy):
            cols = pl.ds(pl.multiple_of((4 * yy + g) * STEP, 128), STEP)

            def side(n):
                return gat[n, yy, pl.ds(4 * g, 4)].reshape(STEP, 128)

            acch[...] += dot_nn(w13t[:, cols], jnp.concatenate([side(0), side(1)], axis=1))
            accq[...] += dot_nn(w2[:, cols], jnp.concatenate([side(2), side(3)], axis=1))

        loop(0, NY, one)

    acch[...] = jnp.zeros_like(acch)
    accq[...] = jnp.zeros_like(accq)

    def at_tick(t, lag, body):
        @pl.when((t >= lag) & (t < lag + 8))
        def _():
            body(t - lag)

    def gather_tick(t):
        at_tick(t, 0, narrow_start)
        at_tick(t, 2, narrow_pass)
        at_tick(t, 4, wide_start)
        at_tick(t, 6, wide_pass)
        at_tick(t, 8, wide_end)
        at_tick(t, 9, core_end)
        at_tick(t, 0, lambda s: loop(24 + 3 * s, 24 + 3 * s + 3, flip))

        @pl.when((t >= 9) & (lax.rem(t, 2) == 0))
        def _():
            project(t - 9)

        @pl.when(t == 6)
        def _():
            sum_middle(0)

        @pl.when(t == 9)
        def _():
            sum_last(0)

    loop(0, 17, gather_tick)

    low_sums = sum_done(0)
    u1 = low_sums[0:16].astype(BF16)
    u3 = low_sums[16:32].astype(BF16)
    v = low_sums[32:48]
    h1 = acch[0:HID] + SCALE * dot_tn(b1[0], u1)
    h3 = acch[HID : 2 * HID] + SCALE * dot_tn(b3[0], u3)
    q = accq[...] + SCALE * dot_tn(d1t[0], v.astype(BF16))
    sig = jax.nn.sigmoid(h1)
    active = h1 * sig
    slope = sig * (1.0 + h1 * (1.0 - sig))
    hidden = (active * h3).astype(BF16)
    back = weight * q
    e1 = (back * h3 * slope).astype(BF16)
    e3 = (back * active).astype(BF16)
    kk = jnp.sum(hidden.astype(F32) * q, axis=0, keepdims=True)
    et[0:HID, :] = e1
    et[HID : 2 * HID, :] = e3
    sum_start(
        1,
        jnp.concatenate(
            [
                dot_nn(b1[0], e1),
                dot_nn(b3[0], e3),
                dot_nn(d1t[0], hidden),
                kk,
                jnp.zeros((15, NT), F32),
            ],
            axis=0,
        ),
    )

    def group_at(s):
        return lax.rem(group + 2 + s + (s // 2) * (1 - 2 * s), 4)

    def piece_z(s, k, core):
        return 4 * group_at(s) + 2 * core + k

    def k_copy(s, core):
        return remote(
            yb.at[:, :, pl.ds(piece_z(s, 0, core), 2)], rc.at[s], k_ss.at[s], k_rs.at[s], sib
        )

    def grads(s):
        g = group_at(s)

        def one(yy):
            rows = pl.ds(pl.multiple_of((4 * yy + g) * STEP, STEP), STEP)
            pair = jnp.concatenate([w1[rows, :], w3[rows, :]], axis=1)
            out = dot_nn(pair, et[...]).astype(BF16).reshape(4, 2, HR, NT)
            for rh in range(2):
                for th in range(2):
                    yb[2 * rh + th, yy, pl.ds(4 * g, 4)] = out[:, rh, :, 128 * th : 128 * th + 128]

        loop(0, NY, one)
        k_copy(s, 1 - c).start()

    def xo_copy(s):
        return remote(
            yb.at[far_x, :, piece_z(s, 0, c)], axo.at[s], p1_ss.at[0], p1_rs.at[0, s], at_x(ahead_x)
        )

    def yo_copy(s):
        return remote(
            yb.at[:, far_y, piece_z(s, 1, c)], byo.at[s], p1_ss.at[0], p1_rs.at[1, s], at_y(ahead_y)
        )

    def xr_copy(k, s, to):
        return remote(
            yb.at[to, :, piece_z(s, 0, c)], axr.at[k, s], p1_ss.at[0], p1_rs.at[2, s], at_x(to)
        )

    def yr_copy(k, s, to):
        return remote(
            yb.at[:, to, piece_z(s, 1, c)], byr.at[k, s], p1_ss.at[0], p1_rs.at[3, s], at_y(to)
        )

    def add_core(s):
        k_copy(s, 1 - c).wait()

        def one(xx):
            zs = pl.ds(piece_z(s, 0, c), 2)
            both = yb[xx, :, zs].astype(F32) + rc[s, xx].astype(F32)
            yb[xx, :, zs] = both.astype(BF16)

        loop(0, NX, one)
        xo_copy(s).start()
        yo_copy(s).start()
        xr_copy(1, s, behind_x).start()
        yr_copy(1, s, behind_y).start()

    def add_far(s):
        za = piece_z(s, 0, c)
        zb = piece_z(s, 1, c)
        xo_copy(s).wait_recv()
        yb[ahead_x, :, za] = (yb[ahead_x, :, za].astype(F32) + axo[s].astype(F32)).astype(BF16)
        xr_copy(0, s, ahead_x).start()
        yo_copy(s).wait_recv()
        yb[:, ahead_y, zb] = (yb[:, ahead_y, zb].astype(F32) + byo[s].astype(F32)).astype(BF16)
        yr_copy(0, s, ahead_y).start()

    def qy_copy(s, i):
        to = lax.rem(y + i, NY)
        return remote(ya.at[s, to], ayb.at[s, i], p2_ss.at[0], p2_rs.at[0, s], at_y(to))

    def qx_copy(s, i):
        to = lax.rem(x + i, NX)
        return remote(yc.at[s, to], bxb.at[s, i], p2_ss.at[0], p2_rs.at[1, s], at_x(to))

    def add_first(s):
        arrived(pieces(8), p1_rs.at[2, s])
        ya[s] = (
            yb[x, :, piece_z(s, 0, c)].astype(F32) + axr[0, s].astype(F32) + axr[1, s].astype(F32)
        ).astype(BF16)
        for i in (2, 1, 3):
            qy_copy(s, i).start()
        arrived(pieces(8), p1_rs.at[3, s])
        yc[s] = (
            yb[:, y, piece_z(s, 1, c)].astype(F32) + byr[0, s].astype(F32) + byr[1, s].astype(F32)
        ).astype(BF16)
        for i in (2, 1, 3):
            qx_copy(s, i).start()

    def t_copy(s, k):
        to = piece_z(s, k, c)
        return remote(zsend.at[s, k], zr.at[z], p3_ss.at[0], p3_rs.at[0], at_z(to))

    def add_second(s):
        for k in range(2):
            arrived(pieces(3), p2_rs.at[k, s])
            piece = (ya[s, y] if k == 0 else yc[s, x]).astype(F32)
            for i in (1, 2, 3):
                piece = piece + (ayb[s, i] if k == 0 else bxb[s, i]).astype(F32)
            zsend[s, k] = piece.astype(BF16)
            to = piece_z(s, k, c)

            @pl.when(to != z)
            def _():
                t_copy(s, k).start()

            @pl.when(to == z)
            def _():
                zr[z] = zsend[s, k]

    def at_step(t, lag, body):
        @pl.when((t >= lag) & (t < lag + 4))
        def _():
            body(t - lag)

    def scatter_tick(t):
        at_step(t, 0, grads)
        at_step(t, 4, add_second)
        at_step(t, 3, add_first)
        at_step(t, 2, add_far)
        at_step(t, 1, add_core)

        @pl.when(t == 3)
        def _():
            sum_middle(1)

        @pl.when(t == 4)
        def _():
            dft[0] = SCALE * dot_nt((weight * v).astype(BF16), hidden)
            gs[0] = SCALE * dot_nt(u1, e1)
            us[0] = SCALE * dot_nt(u3, e3)

        @pl.when(t == 5)
        def _():
            sum_last(1)

    loop(0, 8, scatter_tick)

    holder = lax.rem(z, 4) // 2 == c
    sums = sum_done(1)
    r13 = sums[0:32].astype(BF16)
    zt = (weight * sums[32:48]).astype(BF16)
    ascr[FD:128, :] = jnp.zeros((128 - FD, NT), F32)
    ascr[0:FD, :] = SCALE * dot_tn(a13t, r13)
    ascr[FD : FD + 1, :] = sums[48:49]
    asend[...] = jnp.transpose(ascr[...]).astype(BF16).reshape(8, TB, 128)
    afin[e] = asend[e]

    def h_copy(i, slot):
        to = lax.rem(e + i, 8)
        return remote(asend.at[to], afin.at[slot], h_ss.at[0], h_rs.at[0], (to, j))

    loop(1, 8, lambda i: h_copy(i, e).start())
    first = SCALE * dot_nt(r13, xj[...])
    gft[0] = first[0:16]
    uft[0] = first[16:32]
    ds[0] = SCALE * dot_nt(zt, gj[...])

    rh = x // 2
    th = lax.rem(x, 2)

    def f_copy(i):
        return remote(fsend.at[i], fin.at[rh], f_ss.at[i], f_rs.at[rh], (4 * th + i, j))

    @pl.when(holder)
    def _():
        arrived(pieces(NZ - 1), p3_rs.at[0])
        fscr[...] = jnp.zeros_like(fscr)
        fscr[pl.ds(pl.multiple_of(HR * rh, HR), HR), :] = jnp.sum(zr[...].astype(F32), axis=0)
        fsend[...] = jnp.transpose(fscr[...]).astype(BF16).reshape(4, TB, 128)
        for i in range(4):

            @pl.when(4 * th + i == e)
            def _():
                fin[rh] = fsend[i]

            @pl.when(4 * th + i != e)
            def _():
                f_copy(i).start()

    arrived(afin.at[0:7], h_rs.at[0])

    total = jnp.zeros((TB, 128), F32)
    first_k = jnp.zeros((TB, 1), F32)
    second_k = jnp.zeros((TB, 1), F32)
    for n in range(8):
        block = afin[n].astype(F32)
        total = total + block
        column = block[:, FD : FD + 1]
        first_k = first_k + jnp.where(id0 == n, column, 0.0)
        second_k = second_k + jnp.where(id1 == n, column, 0.0)
    lane = lax.broadcasted_iota(jnp.int32, (TB, 128), 1)
    both_k = jnp.where(lane == 0, first_k, 0.0) + jnp.where(lane == 1, second_k, 0.0)
    cg[...] = jnp.transpose(both_k)[0:2, :]

    for n in range(2):

        @pl.when(4 * n + 2 * (e // 4) + lax.rem(z, 4) // 2 != e)
        def _():
            remote(fsend.at[0], fin.at[n], f_ss.at[0], f_rs.at[n], (e, j)).wait_recv()

    total = total + fin[0].astype(F32) + fin[1].astype(F32)
    tg[...] = total[:, 0:FD].astype(BF16)

    @pl.when(holder)
    def _():
        for i in range(4):

            @pl.when(4 * th + i != e)
            def _():
                f_copy(i).wait_send()

    left(disp.at[0:7], d_ss.at[0])
    left(pieces(NZ - 1), z_ss.at[0])
    left(gat.at[0, :, 0:6], n_ss.at[0])
    left(gat.at[:, :, 0:6], w_ss.at[0])
    left(gat.at[:, :, :, 0], c_ss.at[0])
    for n in range(2):
        left(rsb.at[n, 0 : NZ - 1], r_ss.at[n])
        left(yrec.at[n, 0 : NY - 1], y_ss.at[n])
        left(full.at[n, 0 : NZ - 1], g_ss.at[n])
    left(yb.at[:, :, 0:6], p1_ss.at[0])
    left(gat.at[0, 0:2, 0:12, 0], p2_ss.at[0])
    left(afin.at[0:7], h_ss.at[0])

    @pl.when(holder)
    def _():
        left(pieces(7), p3_ss.at[0])

    @pl.when(jnp.logical_not(holder))
    def _():
        left(pieces(8), p3_ss.at[0])


def finish(*refs):
    sems = refs[16]
    copies = [pltpu.make_async_copy(refs[n], refs[8 + n], sems.at[n]) for n in range(8)]
    for copy in copies:
        copy.start()
    for copy in copies:
        copy.wait()


def local(
    tokens,
    upstream,
    expert_ids,
    slot_pos,
    combine,
    gate_weight,
    upward_weight,
    down_weight,
    gate_adapter_first,
    gate_adapter_second,
    upward_adapter_first,
    upward_adapter_second,
    down_adapter_first,
    down_right,
):
    vmem = pl.BlockSpec(memory_space=pltpu.VMEM)
    hbm = pl.BlockSpec(memory_space=pl.ANY)
    dma = pltpu.SemaphoreType.DMA

    def buf(shape, dtype=BF16):
        return pltpu.VMEM(shape, dtype)

    outs = pl.pallas_call(
        kernel,
        out_shape=(
            jax.ShapeDtypeStruct((TB, FD), BF16),
            jax.ShapeDtypeStruct((2, TB), F32),
            jax.ShapeDtypeStruct((1, 16, FD), F32),
            jax.ShapeDtypeStruct((1, 16, HID), F32),
            jax.ShapeDtypeStruct((1, 16, FD), F32),
            jax.ShapeDtypeStruct((1, 16, HID), F32),
            jax.ShapeDtypeStruct((1, 16, HID), F32),
            jax.ShapeDtypeStruct((1, 16, FD), F32),
        ),
        in_specs=[hbm] * 13,
        out_specs=[vmem] * 8,
        scratch_shapes=[
            buf((TB, FD)),
            buf((TB, FD)),
            buf((2, TB), jnp.int32),
            buf((2, TB), F32),
            buf((1, 16, FD)),
            buf((1, 16, HID)),
            buf((1, 16, FD)),
            buf((1, 16, HID)),
            buf((1, 16, HID)),
            buf((1, 16, FD)),
            buf((6144, HID)),
            buf((6144, HID)),
            buf((HID, 6144)),
            buf((2 * HID, 6144)),
            buf((128, 128), F32),
            buf((2 * TB, 128)),
            buf((8, 2 * TB, 128)),
            buf((FD, NT)),
            buf((FD, NT)),
            buf((NX, NC, HR, 128)),
            buf((NX, NY, NZ, NC, HR, 128)),
            buf((2 * HID, NT), F32),
            buf((HID, NT), F32),
            buf((2 * HID, NT)),
            buf((2, NZ, 8, 128), F32),
            buf((2, NZ, 8, 128), F32),
            buf((2, 8, 128), F32),
            buf((2, NY, 8, 128), F32),
            buf((2, NZ, 8, 128), F32),
            buf((NX, NY, NZ, HR, 128)),
            buf((4, NX, NY, 2, HR, 128)),
            buf((4, NY, HR, 128)),
            buf((4, NX, HR, 128)),
            buf((2, 4, NY, HR, 128)),
            buf((2, 4, NX, HR, 128)),
            buf((4, NY, HR, 128)),
            buf((4, NX, HR, 128)),
            buf((4, 4, HR, 128)),
            buf((4, 4, HR, 128)),
            buf((4, 2, HR, 128)),
            buf((NZ, HR, 128)),
            buf((128, 128), F32),
            buf((4, TB, 128)),
            buf((2, TB, 128)),
            buf((128, NT), F32),
            buf((8, TB, 128)),
            buf((8, TB, 128)),
            dma((13,)),
            dma((1,)),
            dma((1,)),
            dma((1,)),
            dma((NZ,)),
            dma((1,)),
            dma((2, 8)),
            dma((1,)),
            dma((2, 8)),
            dma((1,)),
            dma((8,)),
            dma((2,)),
            dma((2,)),
            dma((2,)),
            dma((2,)),
            dma((2,)),
            dma((2,)),
            dma((4,)),
            dma((4,)),
            dma((1,)),
            dma((4, 4)),
            dma((1,)),
            dma((2, 4)),
            dma((1,)),
            dma((1,)),
            dma((4,)),
            dma((2,)),
            dma((1,)),
            dma((1,)),
            pltpu.SemaphoreType.REGULAR,
        ],
        compiler_params=pltpu.CompilerParams(
            collective_id=0, has_side_effects=True, vmem_limit_bytes=GRANT
        ),
        name="moe_backward",
    )(
        tokens,
        upstream,
        jnp.transpose(expert_ids),
        jnp.transpose(combine),
        gate_weight,
        upward_weight,
        down_weight,
        jnp.swapaxes(gate_adapter_first, 1, 2),
        gate_adapter_second,
        jnp.swapaxes(upward_adapter_first, 1, 2),
        upward_adapter_second,
        jnp.swapaxes(down_adapter_first, 1, 2),
        down_right,
    )
    token_grads, combine_grads, gft, gs, uft, us, dft, ds = pl.pallas_call(
        finish,
        out_shape=[jax.ShapeDtypeStruct(o.shape, o.dtype) for o in outs],
        in_specs=[hbm] * 8,
        out_specs=[hbm] * 8,
        scratch_shapes=[dma((8,))],
        compiler_params=pltpu.CompilerParams(vmem_limit_bytes=GRANT),
        name="hand_over",
    )(*outs)
    return (
        token_grads,
        jnp.transpose(combine_grads),
        jnp.swapaxes(gft, 1, 2),
        gs,
        jnp.swapaxes(uft, 1, 2),
        us,
        jnp.swapaxes(dft, 1, 2),
        ds,
    )


def solution(mesh):
    in_specs = (
        P("expert", "tensor"),
        P("expert", "tensor"),
        P("expert", None),
        P("expert", None),
        P("expert", None),
        P("expert", None, "tensor"),
        P("expert", None, "tensor"),
        P("expert", "tensor", None),
        P("expert", "tensor", None),
        P("expert", None, "tensor"),
        P("expert", "tensor", None),
        P("expert", None, "tensor"),
        P("expert", "tensor", None),
        P("expert", None, "tensor"),
    )
    out_specs = (
        P("expert", "tensor"),
        P("expert", None),
        P("expert", "tensor", None),
        P("expert", None, "tensor"),
        P("expert", "tensor", None),
        P("expert", None, "tensor"),
        P("expert", "tensor", None),
        P("expert", None, "tensor"),
    )
    return jax.shard_map(local, mesh=mesh, in_specs=in_specs, out_specs=out_specs, check_vma=False)
```

```python
import jax
import jax.numpy as jnp
from jax import lax
from jax.experimental import pallas as pl
from jax.experimental.pallas import tpu as pltpu
from jax.sharding import PartitionSpec as P

MESH = pl.DeviceIdType.MESH
F32 = jnp.float32
BF16 = jnp.bfloat16
SCALE = 2.0
NX, NY, NZ, NC = 4, 4, 16, 2
TB = 32
FD = 96
HR = 48
HID = 128
NT = 256
STEP = 4 * FD
GRANT = 60 * 2**20
NEAR = 4


def dot_nn(a, b):
    return lax.dot_general(a, b, (((1,), (0,)), ((), ())), preferred_element_type=F32)


def dot_nt(a, b):
    return lax.dot_general(a, b, (((1,), (1,)), ((), ())), preferred_element_type=F32)


def dot_tn(a, b):
    return lax.dot_general(a, b, (((0,), (0,)), ((), ())), preferred_element_type=F32)


def remote(src, dst, send, recv, dev):
    return pltpu.make_async_remote_copy(
        src_ref=src, dst_ref=dst, send_sem=send, recv_sem=recv, device_id=dev, device_id_type=MESH
    )


def loop(low, high, body):
    def step(i, carry):
        body(i)
        return carry

    lax.fori_loop(low, high, step, 0)


def kernel(
    tok_hbm,
    ups_hbm,
    ids_hbm,
    comb_hbm,
    w1_hbm,
    w3_hbm,
    w2_hbm,
    a1t_hbm,
    b1_hbm,
    a3t_hbm,
    b3_hbm,
    d1t_hbm,
    rj_hbm,
    tg,
    cg,
    gft,
    gs,
    uft,
    us,
    dft,
    ds,
    tok,
    ups,
    ids,
    comb,
    a1t,
    b1,
    a3t,
    b3,
    d1t,
    rj,
    w1,
    w3,
    w2,
    w13t,
    wide_t,
    src,
    disp,
    xj,
    gj,
    own,
    gat,
    acch,
    accq,
    et,
    part,
    rsb,
    ysend,
    yrec,
    full,
    yb,
    rc,
    axo,
    byo,
    axr,
    byr,
    ya,
    yc,
    ayb,
    bxb,
    zsend,
    zr,
    fscr,
    fsend,
    fin,
    ascr,
    asend,
    afin,
    w_sem,
    d_ss,
    d_rs,
    z_ss,
    z_rs,
    n_ss,
    n_rs,
    w_ss,
    w_rs,
    c_ss,
    c_rs,
    r_ss,
    r_rs,
    y_ss,
    y_rs,
    g_ss,
    g_rs,
    k_ss,
    k_rs,
    p1_ss,
    p1_rs,
    p2_ss,
    p2_rs,
    p3_ss,
    p3_rs,
    f_ss,
    f_rs,
    h_ss,
    h_rs,
    known,
):
    e = lax.axis_index("expert")
    j = lax.axis_index("tensor")
    x = e // 2
    c = lax.rem(e, 2)
    y = j // NZ
    z = lax.rem(j, NZ)
    sib = (2 * x + 1 - c, j)

    def at_x(v):
        return (2 * v + c, j)

    def at_y(v):
        return (e, v * NZ + z)

    def at_z(v):
        return (e, y * NZ + v)

    def arrived(ref, sem):
        remote(ref, ref, sem, sem, sib).wait_recv()

    def left(ref, sem):
        remote(ref, ref, sem, sem, sib).wait_send()

    def pieces(n):
        return gat.at[0, 0, 0:n, 0]

    bar = pltpu.get_barrier_semaphore()

    def sig_e(i):
        pl.semaphore_signal(bar, inc=1, device_id=(lax.rem(e + i, 8), j), device_id_type=MESH)

    def sig_z(i):
        pl.semaphore_signal(bar, inc=1, device_id=at_z(lax.rem(z + i, NZ)), device_id_type=MESH)

    def sig_y(i):
        pl.semaphore_signal(bar, inc=1, device_id=at_y(lax.rem(y + i, NY)), device_id_type=MESH)

    loop(1, NEAR + 1, sig_z)
    loop(NZ - NEAR, NZ, sig_z)
    loop(1, NY, sig_y)
    loop(1, 8, sig_e)

    pairs = [
        (tok_hbm, tok),
        (ups_hbm, ups),
        (ids_hbm, ids),
        (comb_hbm, comb),
        (a1t_hbm, a1t),
        (b1_hbm, b1),
        (a3t_hbm, a3t),
        (b3_hbm, b3),
        (d1t_hbm, d1t),
        (rj_hbm, rj),
        (w1_hbm.at[0], w1),
        (w3_hbm.at[0], w3),
        (w2_hbm.at[0], w2),
    ]
    loads = [pltpu.make_async_copy(a, b, w_sem.at[n]) for n, (a, b) in enumerate(pairs)]
    for load in loads:
        load.start()
    for load in loads[0:4]:
        load.wait()

    expert_row = lax.broadcasted_iota(jnp.int32, (8, TB), 0)
    dense = jnp.zeros((8, TB), F32)
    for k in range(2):
        dense = dense + jnp.where(expert_row == ids[k : k + 1, :], comb[k : k + 1, :], 0.0)
    high = dense.astype(BF16).astype(F32)
    wide_t[...] = jnp.zeros_like(wide_t)
    wide_t[0:2, 0:TB] = ids[...].astype(F32)
    wide_t[FD : FD + 8, 0:TB] = high
    wide_t[FD + 8 : FD + 16, 0:TB] = dense - high
    wide = jnp.transpose(wide_t[...])[0:TB, :]
    id0 = wide[:, 0:1]
    id1 = wide[:, 1:2]
    src[0:TB, :] = wide.astype(BF16)
    src[0:TB, 0:FD] = tok[...]
    src[TB : 2 * TB, :] = jnp.zeros((TB, 128), BF16)
    src[TB : 2 * TB, 0:FD] = ups[...]
    disp[e] = src[...]
    for load in loads[4:]:
        load.wait()

    def flip(i):
        rows = pl.ds(pl.multiple_of(i * 128, 128), 128)
        w13t[0:HID, rows] = jnp.transpose(w1[rows, :])
        w13t[HID : 2 * HID, rows] = jnp.transpose(w3[rows, :])


    loop(0, 24, flip)
    pl.semaphore_wait(bar, 7 + 2 * NEAR + NY - 1)

    def disp_copy(i, slot):
        return remote(
            src, disp.at[slot], d_ss.at[0], d_rs.at[0], (lax.rem(e + i, 8), j)
        )

    loop(1, 8, lambda i: disp_copy(i, e).start())
    for step in (NEAR, NZ - NEAR):
        pl.semaphore_signal(
            known, inc=1, device_id=at_z(lax.rem(z + step, NZ)), device_id_type=MESH
        )
    arrived(disp.at[0:7], d_rs.at[0])

    xt = jnp.transpose(disp[:, 0:TB, :].reshape(NT, 128))
    gt = jnp.transpose(disp[:, TB : 2 * TB, :].reshape(NT, 128))
    row = lax.broadcasted_iota(jnp.int32, (32, NT), 0)
    tail = xt[FD:128, :].astype(F32)
    weight = jnp.sum(jnp.where((row == e) | (row == e + 8), tail, 0.0), axis=0, keepdims=True)
    xj[...] = xt[0:FD, :]
    gj[...] = gt[0:FD, :]
    for half in range(2):
        for th in range(2):
            cut = slice(128 * th, 128 * th + 128)
            rows = slice(HR * half, HR * half + HR)
            own[th, half] = xt[rows, cut]
            own[2 + th, half] = gt[rows, cut]
    gat[x, y, z, c] = own[x, c]

    pl.semaphore_wait(known, 2)

    def z_copy(of, to):
        piece = gat.at[x, y, of, c]
        return remote(piece, piece, z_ss.at[0], z_rs.at[of], at_z(to))

    group = z // 4
    for off in (0, 3, 1, 2):

        def z_start(i):
            to = 4 * lax.rem(group + off, 4) + i

            @pl.when(to != z)
            def _():
                z_copy(z, to).start()

        loop(0, 4, z_start)

    def sum_start(n, value):
        for k in range(NZ):
            part[n, k] = value[8 * (k // 2) : 8 * (k // 2) + 8, 128 * (k % 2) : 128 * (k % 2) + 128]
        rsb[n, z] = part[n, z]

        def go(i):
            to = lax.rem(z + i, NZ)
            remote(part.at[n, to], rsb.at[n, z], r_ss.at[n], r_rs.at[n], at_z(to)).start()

        loop(1, NZ, go)

    def y_copy(n, i, slot):
        return remote(
            ysend.at[n], yrec.at[n, slot], y_ss.at[n], y_rs.at[n], at_y(lax.rem(y + i, NY))
        )

    def sum_middle(n):
        arrived(rsb.at[n, 0 : NZ - 1], r_rs.at[n])
        total = jnp.sum(rsb[n], axis=0)
        ysend[n] = total
        yrec[n, y] = total
        loop(1, NY, lambda i: y_copy(n, i, y).start())

    def g_copy(n, i, slot):
        piece = full.at[n, slot]
        return remote(piece, piece, g_ss.at[n], g_rs.at[n], at_z(lax.rem(z + i, NZ)))

    def sum_last(n):
        arrived(yrec.at[n, 0 : NY - 1], y_rs.at[n])
        full[n, z] = jnp.sum(yrec[n], axis=0)
        loop(1, NZ, lambda i: g_copy(n, i, z).start())

    def sum_done(n):
        arrived(full.at[n, 0 : NZ - 1], g_rs.at[n])
        return jnp.concatenate(
            [jnp.concatenate([full[n, 2 * k], full[n, 2 * k + 1]], axis=1) for k in range(8)], axis=0
        )

    a13t = jnp.concatenate([a1t[0], a3t[0]], axis=0)
    sum_start(
        0,
        jnp.concatenate(
            [dot_nn(a13t, xj[...]), dot_nn(rj[0], gj[...]), jnp.zeros((16, NT), F32)], axis=0
        ),
    )

    ahead_x = lax.rem(x + 1 + 2 * c, NX)
    behind_x = lax.rem(x + 3 + 2 * c, NX)
    far_x = lax.rem(x + 2, NX)
    ahead_y = lax.rem(y + 1 + 2 * c, NY)
    behind_y = lax.rem(y + 3 + 2 * c, NY)
    far_y = lax.rem(y + 2, NY)

    def group_of(s):
        n = s // 2
        return lax.rem(group + n + n // 2 - 2 * (n // 3), 4)

    def z_of(s, k):
        return 4 * group_of(s) + 2 * lax.rem(s, 2) + k

    def a1_copy(k, s, of, to):
        piece = gat.at[of, y, z_of(s, 0), c]
        return remote(piece, piece, n_ss.at[0], n_rs.at[(k + 1) // 2, s], at_x(to))

    def b1_copy(k, s, of, to):
        piece = gat.at[x, of, z_of(s, 1), c]
        return remote(piece, piece, n_ss.at[0], n_rs.at[(k + 1) // 2, s], at_y(to))

    def a2_copy(k, s, of, to):
        piece = gat.at[:, of, z_of(s, 0), c]
        return remote(piece, piece, w_ss.at[0], w_rs.at[(k + 1) // 2, s], at_y(to))

    def b2_copy(k, s, of, to):
        piece = gat.at[of, :, z_of(s, 1), c]
        return remote(piece, piece, w_ss.at[0], w_rs.at[(k + 1) // 2, s], at_x(to))

    def core_copy(s):
        piece = gat.at[:, :, pl.ds(z_of(s, 0), 2), c]
        return remote(piece, piece, c_ss.at[0], c_rs.at[s], sib)

    def narrow_start(s):
        for k in range(2):
            of = z_of(s, k)

            @pl.when(of != z)
            def _():
                z_copy(of, z).wait_recv()

        a1_copy(0, s, x, ahead_x).start()
        b1_copy(0, s, y, ahead_y).start()
        a1_copy(1, s, x, behind_x).start()
        b1_copy(1, s, y, behind_y).start()

    def narrow_pass(s):
        arrived(pieces(2), n_rs.at[0, s])
        a1_copy(2, s, behind_x, ahead_x).start()
        b1_copy(2, s, behind_y, ahead_y).start()

    def wide_start(s):
        arrived(pieces(4), n_rs.at[1, s])
        a2_copy(0, s, y, ahead_y).start()
        b2_copy(0, s, x, ahead_x).start()
        a2_copy(1, s, y, behind_y).start()
        b2_copy(1, s, x, behind_x).start()

    def wide_pass(s):
        arrived(pieces(8), w_rs.at[0, s])
        a2_copy(2, s, behind_y, ahead_y).start()
        b2_copy(2, s, behind_x, ahead_x).start()

    def wide_end(s):
        arrived(pieces(16), w_rs.at[1, s])
        core_copy(s).start()

    def core_end(s):
        core_copy(s).wait_recv()

    def project(s):
        g = group_of(s)

        def one(yy):
            cols = pl.ds(pl.multiple_of((4 * yy + g) * STEP, 128), STEP)

            def side(n):
                return gat[n, yy, pl.ds(4 * g, 4)].reshape(STEP, 128)

            acch[...] += dot_nn(w13t[:, cols], jnp.concatenate([side(0), side(1)], axis=1))
            accq[...] += dot_nn(w2[:, cols], jnp.concatenate([side(2), side(3)], axis=1))

        loop(0, NY, one)

    acch[...] = jnp.zeros_like(acch)
    accq[...] = jnp.zeros_like(accq)

    def at_tick(t, lag, body):
        @pl.when((t >= lag) & (t < lag + 8))
        def _():
            body(t - lag)

    def gather_tick(t):
        at_tick(t, 0, narrow_start)
        at_tick(t, 2, narrow_pass)
        at_tick(t, 4, wide_start)
        at_tick(t, 6, wide_pass)
        at_tick(t, 8, wide_end)
        at_tick(t, 9, core_end)
        at_tick(t, 0, lambda s: loop(24 + 3 * s, 24 + 3 * s + 3, flip))

        @pl.when((t >= 9) & (lax.rem(t, 2) == 0))
        def _():
            project(t - 9)

        @pl.when(t == 6)
        def _():
            sum_middle(0)

        @pl.when(t == 9)
        def _():
            sum_last(0)

    loop(0, 17, gather_tick)

    low_sums = sum_done(0)
    u1 = low_sums[0:16].astype(BF16)
    u3 = low_sums[16:32].astype(BF16)
    v = low_sums[32:48]
    h1 = acch[0:HID] + SCALE * dot_tn(b1[0], u1)
    h3 = acch[HID : 2 * HID] + SCALE * dot_tn(b3[0], u3)
    q = accq[...] + SCALE * dot_tn(d1t[0], v.astype(BF16))
    sig = jax.nn.sigmoid(h1)
    active = h1 * sig
    slope = sig * (1.0 + h1 * (1.0 - sig))
    hidden = (active * h3).astype(BF16)
    back = weight * q
    e1 = (back * h3 * slope).astype(BF16)
    e3 = (back * active).astype(BF16)
    kk = jnp.sum(hidden.astype(F32) * q, axis=0, keepdims=True)
    et[0:HID, :] = e1
    et[HID : 2 * HID, :] = e3
    sum_start(
        1,
        jnp.concatenate(
            [
                dot_nn(b1[0], e1),
                dot_nn(b3[0], e3),
                dot_nn(d1t[0], hidden),
                kk,
                jnp.zeros((15, NT), F32),
            ],
            axis=0,
        ),
    )

    def group_at(s):
        return lax.rem(group + 2 + s + (s // 2) * (1 - 2 * s), 4)

    def piece_z(s, k, core):
        return 4 * group_at(s) + 2 * core + k

    def k_copy(s, core):
        return remote(
            yb.at[:, :, pl.ds(piece_z(s, 0, core), 2)], rc.at[s], k_ss.at[s], k_rs.at[s], sib
        )

    def grads(s):
        g = group_at(s)

        def one(yy):
            rows = pl.ds(pl.multiple_of((4 * yy + g) * STEP, STEP), STEP)
            pair = jnp.concatenate([w1[rows, :], w3[rows, :]], axis=1)
            out = dot_nn(pair, et[...]).astype(BF16).reshape(4, 2, HR, NT)
            for rh in range(2):
                for th in range(2):
                    yb[2 * rh + th, yy, pl.ds(4 * g, 4)] = out[:, rh, :, 128 * th : 128 * th + 128]

        loop(0, NY, one)
        k_copy(s, 1 - c).start()

    def xo_copy(s):
        return remote(
            yb.at[far_x, :, piece_z(s, 0, c)], axo.at[s], p1_ss.at[0], p1_rs.at[0, s], at_x(ahead_x)
        )

    def yo_copy(s):
        return remote(
            yb.at[:, far_y, piece_z(s, 1, c)], byo.at[s], p1_ss.at[0], p1_rs.at[1, s], at_y(ahead_y)
        )

    def xr_copy(k, s, to):
        return remote(
            yb.at[to, :, piece_z(s, 0, c)], axr.at[k, s], p1_ss.at[0], p1_rs.at[2, s], at_x(to)
        )

    def yr_copy(k, s, to):
        return remote(
            yb.at[:, to, piece_z(s, 1, c)], byr.at[k, s], p1_ss.at[0], p1_rs.at[3, s], at_y(to)
        )

    def add_core(s):
        k_copy(s, 1 - c).wait()

        def one(xx):
            zs = pl.ds(piece_z(s, 0, c), 2)
            both = yb[xx, :, zs].astype(F32) + rc[s, xx].astype(F32)
            yb[xx, :, zs] = both.astype(BF16)

        loop(0, NX, one)
        xo_copy(s).start()
        yo_copy(s).start()
        xr_copy(1, s, behind_x).start()
        yr_copy(1, s, behind_y).start()

    def add_far(s):
        za = piece_z(s, 0, c)
        zb = piece_z(s, 1, c)
        xo_copy(s).wait_recv()
        yb[ahead_x, :, za] = (yb[ahead_x, :, za].astype(F32) + axo[s].astype(F32)).astype(BF16)
        xr_copy(0, s, ahead_x).start()
        yo_copy(s).wait_recv()
        yb[:, ahead_y, zb] = (yb[:, ahead_y, zb].astype(F32) + byo[s].astype(F32)).astype(BF16)
        yr_copy(0, s, ahead_y).start()

    def qy_copy(s, i):
        to = lax.rem(y + i, NY)
        return remote(ya.at[s, to], ayb.at[s, i], p2_ss.at[0], p2_rs.at[0, s], at_y(to))

    def qx_copy(s, i):
        to = lax.rem(x + i, NX)
        return remote(yc.at[s, to], bxb.at[s, i], p2_ss.at[0], p2_rs.at[1, s], at_x(to))

    def add_first(s):
        arrived(pieces(8), p1_rs.at[2, s])
        ya[s] = (
            yb[x, :, piece_z(s, 0, c)].astype(F32) + axr[0, s].astype(F32) + axr[1, s].astype(F32)
        ).astype(BF16)
        for i in (2, 1, 3):
            qy_copy(s, i).start()
        arrived(pieces(8), p1_rs.at[3, s])
        yc[s] = (
            yb[:, y, piece_z(s, 1, c)].astype(F32) + byr[0, s].astype(F32) + byr[1, s].astype(F32)
        ).astype(BF16)
        for i in (2, 1, 3):
            qx_copy(s, i).start()

    def t_copy(s, k):
        to = piece_z(s, k, c)
        return remote(zsend.at[s, k], zr.at[z], p3_ss.at[0], p3_rs.at[0], at_z(to))

    def add_second(s):
        for k in range(2):
            arrived(pieces(3), p2_rs.at[k, s])
            piece = (ya[s, y] if k == 0 else yc[s, x]).astype(F32)
            for i in (1, 2, 3):
                piece = piece + (ayb[s, i] if k == 0 else bxb[s, i]).astype(F32)
            zsend[s, k] = piece.astype(BF16)
            to = piece_z(s, k, c)

            @pl.when(to != z)
            def _():
                t_copy(s, k).start()

            @pl.when(to == z)
            def _():
                zr[z] = zsend[s, k]

    def at_step(t, lag, body):
        @pl.when((t >= lag) & (t < lag + 4))
        def _():
            body(t - lag)

    def scatter_tick(t):
        at_step(t, 0, grads)
        at_step(t, 1, add_core)
        at_step(t, 3, add_far)
        at_step(t, 5, add_first)
        at_step(t, 7, add_second)

        @pl.when(t == 5)
        def _():
            sum_middle(1)

        @pl.when(t == 9)
        def _():
            dft[0] = SCALE * dot_nt((weight * v).astype(BF16), hidden)
            gs[0] = SCALE * dot_nt(u1, e1)
            us[0] = SCALE * dot_nt(u3, e3)

        @pl.when(t == 7)
        def _():
            sum_last(1)

    loop(0, 11, scatter_tick)

    holder = lax.rem(z, 4) // 2 == c
    sums = sum_done(1)
    r13 = sums[0:32].astype(BF16)
    zt = (weight * sums[32:48]).astype(BF16)
    ascr[FD:128, :] = jnp.zeros((128 - FD, NT), F32)
    ascr[0:FD, :] = SCALE * dot_tn(a13t, r13)
    ascr[FD : FD + 1, :] = sums[48:49]
    asend[...] = jnp.transpose(ascr[...]).astype(BF16).reshape(8, TB, 128)
    afin[e] = asend[e]

    def h_copy(i, slot):
        to = lax.rem(e + i, 8)
        return remote(asend.at[to], afin.at[slot], h_ss.at[0], h_rs.at[0], (to, j))

    loop(1, 8, lambda i: h_copy(i, e).start())
    first = SCALE * dot_nt(r13, xj[...])
    gft[0] = first[0:16]
    uft[0] = first[16:32]
    ds[0] = SCALE * dot_nt(zt, gj[...])

    rh = x // 2
    th = lax.rem(x, 2)

    def f_copy(i):
        return remote(fsend.at[i], fin.at[rh], f_ss.at[i], f_rs.at[rh], (4 * th + i, j))

    @pl.when(holder)
    def _():
        arrived(pieces(NZ - 1), p3_rs.at[0])
        fscr[...] = jnp.zeros_like(fscr)
        fscr[pl.ds(pl.multiple_of(HR * rh, HR), HR), :] = jnp.sum(zr[...].astype(F32), axis=0)
        fsend[...] = jnp.transpose(fscr[...]).astype(BF16).reshape(4, TB, 128)
        for i in range(4):

            @pl.when(4 * th + i == e)
            def _():
                fin[rh] = fsend[i]

            @pl.when(4 * th + i != e)
            def _():
                f_copy(i).start()

    arrived(afin.at[0:7], h_rs.at[0])

    total = jnp.zeros((TB, 128), F32)
    first_k = jnp.zeros((TB, 1), F32)
    second_k = jnp.zeros((TB, 1), F32)
    for n in range(8):
        block = afin[n].astype(F32)
        total = total + block
        column = block[:, FD : FD + 1]
        first_k = first_k + jnp.where(id0 == n, column, 0.0)
        second_k = second_k + jnp.where(id1 == n, column, 0.0)
    lane = lax.broadcasted_iota(jnp.int32, (TB, 128), 1)
    both_k = jnp.where(lane == 0, first_k, 0.0) + jnp.where(lane == 1, second_k, 0.0)
    cg[...] = jnp.transpose(both_k)[0:2, :]

    for n in range(2):

        @pl.when(4 * n + 2 * (e // 4) + lax.rem(z, 4) // 2 != e)
        def _():
            remote(fsend.at[0], fin.at[n], f_ss.at[0], f_rs.at[n], (e, j)).wait_recv()

    total = total + fin[0].astype(F32) + fin[1].astype(F32)
    tg[...] = total[:, 0:FD].astype(BF16)

    @pl.when(holder)
    def _():
        for i in range(4):

            @pl.when(4 * th + i != e)
            def _():
                f_copy(i).wait_send()

    left(disp.at[0:7], d_ss.at[0])
    left(pieces(NZ - 1), z_ss.at[0])
    left(gat.at[0, :, 0:6], n_ss.at[0])
    left(gat.at[:, :, 0:6], w_ss.at[0])
    left(gat.at[:, :, :, 0], c_ss.at[0])
    for n in range(2):
        left(rsb.at[n, 0 : NZ - 1], r_ss.at[n])
        left(yrec.at[n, 0 : NY - 1], y_ss.at[n])
        left(full.at[n, 0 : NZ - 1], g_ss.at[n])
    left(yb.at[:, :, 0:6], p1_ss.at[0])
    left(gat.at[0, 0:2, 0:12, 0], p2_ss.at[0])
    left(afin.at[0:7], h_ss.at[0])

    @pl.when(holder)
    def _():
        left(pieces(7), p3_ss.at[0])

    @pl.when(jnp.logical_not(holder))
    def _():
        left(pieces(8), p3_ss.at[0])


def finish(*refs):
    sems = refs[16]
    copies = [pltpu.make_async_copy(refs[n], refs[8 + n], sems.at[n]) for n in range(8)]
    for copy in copies:
        copy.start()
    for copy in copies:
        copy.wait()


def local(
    tokens,
    upstream,
    expert_ids,
    slot_pos,
    combine,
    gate_weight,
    upward_weight,
    down_weight,
    gate_adapter_first,
    gate_adapter_second,
    upward_adapter_first,
    upward_adapter_second,
    down_adapter_first,
    down_right,
):
    vmem = pl.BlockSpec(memory_space=pltpu.VMEM)
    hbm = pl.BlockSpec(memory_space=pl.ANY)
    dma = pltpu.SemaphoreType.DMA

    def buf(shape, dtype=BF16):
        return pltpu.VMEM(shape, dtype)

    outs = pl.pallas_call(
        kernel,
        out_shape=(
            jax.ShapeDtypeStruct((TB, FD), BF16),
            jax.ShapeDtypeStruct((2, TB), F32),
            jax.ShapeDtypeStruct((1, 16, FD), F32),
            jax.ShapeDtypeStruct((1, 16, HID), F32),
            jax.ShapeDtypeStruct((1, 16, FD), F32),
            jax.ShapeDtypeStruct((1, 16, HID), F32),
            jax.ShapeDtypeStruct((1, 16, HID), F32),
            jax.ShapeDtypeStruct((1, 16, FD), F32),
        ),
        in_specs=[hbm] * 13,
        out_specs=[vmem] * 8,
        scratch_shapes=[
            buf((TB, FD)),
            buf((TB, FD)),
            buf((2, TB), jnp.int32),
            buf((2, TB), F32),
            buf((1, 16, FD)),
            buf((1, 16, HID)),
            buf((1, 16, FD)),
            buf((1, 16, HID)),
            buf((1, 16, HID)),
            buf((1, 16, FD)),
            buf((6144, HID)),
            buf((6144, HID)),
            buf((HID, 6144)),
            buf((2 * HID, 6144)),
            buf((128, 128), F32),
            buf((2 * TB, 128)),
            buf((8, 2 * TB, 128)),
            buf((FD, NT)),
            buf((FD, NT)),
            buf((NX, NC, HR, 128)),
            buf((NX, NY, NZ, NC, HR, 128)),
            buf((2 * HID, NT), F32),
            buf((HID, NT), F32),
            buf((2 * HID, NT)),
            buf((2, NZ, 8, 128), F32),
            buf((2, NZ, 8, 128), F32),
            buf((2, 8, 128), F32),
            buf((2, NY, 8, 128), F32),
            buf((2, NZ, 8, 128), F32),
            buf((NX, NY, NZ, HR, 128)),
            buf((4, NX, NY, 2, HR, 128)),
            buf((4, NY, HR, 128)),
            buf((4, NX, HR, 128)),
            buf((2, 4, NY, HR, 128)),
            buf((2, 4, NX, HR, 128)),
            buf((4, NY, HR, 128)),
            buf((4, NX, HR, 128)),
            buf((4, 4, HR, 128)),
            buf((4, 4, HR, 128)),
            buf((4, 2, HR, 128)),
            buf((NZ, HR, 128)),
            buf((128, 128), F32),
            buf((4, TB, 128)),
            buf((2, TB, 128)),
            buf((128, NT), F32),
            buf((8, TB, 128)),
            buf((8, TB, 128)),
            dma((13,)),
            dma((1,)),
            dma((1,)),
            dma((1,)),
            dma((NZ,)),
            dma((1,)),
            dma((2, 8)),
            dma((1,)),
            dma((2, 8)),
            dma((1,)),
            dma((8,)),
            dma((2,)),
            dma((2,)),
            dma((2,)),
            dma((2,)),
            dma((2,)),
            dma((2,)),
            dma((4,)),
            dma((4,)),
            dma((1,)),
            dma((4, 4)),
            dma((1,)),
            dma((2, 4)),
            dma((1,)),
            dma((1,)),
            dma((4,)),
            dma((2,)),
            dma((1,)),
            dma((1,)),
            pltpu.SemaphoreType.REGULAR,
        ],
        compiler_params=pltpu.CompilerParams(
            collective_id=0, has_side_effects=True, vmem_limit_bytes=GRANT
        ),
        name="moe_backward",
    )(
        tokens,
        upstream,
        jnp.transpose(expert_ids),
        jnp.transpose(combine),
        gate_weight,
        upward_weight,
        down_weight,
        jnp.swapaxes(gate_adapter_first, 1, 2),
        gate_adapter_second,
        jnp.swapaxes(upward_adapter_first, 1, 2),
        upward_adapter_second,
        jnp.swapaxes(down_adapter_first, 1, 2),
        down_right,
    )
    token_grads, combine_grads, gft, gs, uft, us, dft, ds = pl.pallas_call(
        finish,
        out_shape=[jax.ShapeDtypeStruct(o.shape, o.dtype) for o in outs],
        in_specs=[hbm] * 8,
        out_specs=[hbm] * 8,
        scratch_shapes=[dma((8,))],
        compiler_params=pltpu.CompilerParams(vmem_limit_bytes=GRANT),
        name="hand_over",
    )(*outs)
    return (
        token_grads,
        jnp.transpose(combine_grads),
        jnp.swapaxes(gft, 1, 2),
        gs,
        jnp.swapaxes(uft, 1, 2),
        us,
        jnp.swapaxes(dft, 1, 2),
        ds,
    )


def solution(mesh):
    in_specs = (
        P("expert", "tensor"),
        P("expert", "tensor"),
        P("expert", None),
        P("expert", None),
        P("expert", None),
        P("expert", None, "tensor"),
        P("expert", None, "tensor"),
        P("expert", "tensor", None),
        P("expert", "tensor", None),
        P("expert", None, "tensor"),
        P("expert", "tensor", None),
        P("expert", None, "tensor"),
        P("expert", "tensor", None),
        P("expert", None, "tensor"),
    )
    out_specs = (
        P("expert", "tensor"),
        P("expert", None),
        P("expert", "tensor", None),
        P("expert", None, "tensor"),
        P("expert", "tensor", None),
        P("expert", None, "tensor"),
        P("expert", "tensor", None),
        P("expert", None, "tensor"),
    )
    return jax.shard_map(local, mesh=mesh, in_specs=in_specs, out_specs=out_specs, check_vma=False)
```
